512 devices in a mesh: ctx: 64 (over z, y), head: 8 (over x, core).
Axes of the slice: x: 4, y: 4, z: 16, core: 2. Of those that a mesh axis runs over, the one named last changes fastest.
Arguments:
- query_rows: bfloat16 [65536, 2048], P(('ctx', 'head')), may hold values from -2.5 to 2.5
- key_rows: bfloat16 [65536, 2048], P(('ctx', 'head')), may hold values from -2.5 to 2.5
- value_rows: bfloat16 [65536, 2048], P(('ctx', 'head')), may hold values from -6 to 6
- grad_rows: bfloat16 [65536, 2048], P(('ctx', 'head')), may hold values from -6 to 6
Outputs:
- attended: bfloat16 [65536, 2048], P(('ctx', 'head'))
- grad_query: bfloat16 [65536, 2048], P(('ctx', 'head'))
- grad_key: bfloat16 [65536, 2048], P(('ctx', 'head'))
- grad_value: bfloat16 [65536, 2048], P(('ctx', 'head'))
The draws below stay inside these ranges and needn't reach their ends.
All inputs are finite; a program needn't handle non-finite values.
Results may differ from the reference program's by a relative error of at most 0.0075.
Values may be sent and summed in bfloat16 or wider, within the bound.
No kernel may reach another device: no remote copies, remote signals or barrier semaphores. Data moves between devices by JAX's collectives and lax.ppermute only.
A program may use at most 64 MiB of HBM per device.

```python
import jax
import jax.numpy as jnp
from jax import lax

HEADS = 16
HEAD_DIM = 128
SPAN = 1024
TOKENS = 65536
WIDTH = 2048


def block_scale(stream_key, extent, shards, least, top_value):
    gain = 1.0
    for position, shards_of in shards:
        steps = jax.random.uniform(jax.random.fold_in(jax.random.fold_in(stream_key, 6), position), (shards_of,), jnp.float32, least / len(shards), top_value / len(shards))
        gain = gain * jnp.repeat(jnp.exp(steps), extent[position] // shards_of).reshape((-1,) + (1,) * (len(extent) - 1 - position))
    return gain


def scatter_about(own_key, extent, spread, most, split=(), kind=jnp.bfloat16):
    result = spread * jax.random.normal(own_key, extent, jnp.float32)
    if split:
        result = result * block_scale(own_key, extent, split, -0.22, 0.18)
    return jnp.clip(result, -most, most).astype(kind)


def setup_inputs(seed: int = 0) -> dict:
    arg_keys = jax.random.split(jax.random.key(seed), 5)
    return {
        "query_rows": scatter_about(arg_keys[0], (TOKENS, WIDTH), 0.3, 2.5, ((0, 512),)),
        "key_rows": scatter_about(arg_keys[1], (TOKENS, WIDTH), 0.3, 2.5, ((0, 512),)),
        "value_rows": scatter_about(arg_keys[2], (TOKENS, WIDTH), 1.0, 6.0, ((0, 512),)),
        "grad_rows": scatter_about(arg_keys[3], (TOKENS, WIDTH), 1.0, 6.0, ((0, 512),)),
    }


def causal_mask(count):
    rows = lax.broadcasted_iota(jnp.int32, (count, count), 0)
    cols = lax.broadcasted_iota(jnp.int32, (count, count), 1)
    return rows >= cols

def span_front(query, keys, values, grads, prior):
    prior_bf = prior.astype(jnp.bfloat16)
    mask = causal_mask(query.shape[0])
    scores = jnp.einsum('thd,shd->hts', query.astype(jnp.float32), keys.astype(jnp.float32))
    local = jnp.where(mask[None], scores, 0.0).astype(jnp.bfloat16)
    inner = jnp.einsum('hts,she->the', local.astype(jnp.float32), values.astype(jnp.float32))
    outer = jnp.einsum('thd,hde->the', query.astype(jnp.float32), prior_bf.astype(jnp.float32))
    mixed = inner + outer
    scale = lax.rsqrt(lax.optimization_barrier(jnp.mean(mixed * mixed, axis=-1, keepdims=True)) + 1e-06)
    attended = (mixed * scale).astype(jnp.bfloat16)
    grad_f = grads.astype(jnp.float32)
    inner_mean = lax.optimization_barrier(jnp.mean(grad_f * mixed, axis=-1, keepdims=True))
    dmixed = (scale * grad_f - mixed * scale * scale * scale * inner_mean).astype(jnp.bfloat16)
    state_grad = jnp.einsum('thd,the->hde', query.astype(jnp.float32), dmixed.astype(jnp.float32))
    return (attended, dmixed, state_grad)

def span_back(query, keys, values, dmixed, prior, later):
    prior_bf = prior.astype(jnp.bfloat16).astype(jnp.float32)
    later_bf = later.astype(jnp.bfloat16).astype(jnp.float32)
    mask = causal_mask(query.shape[0])
    qf = query.astype(jnp.float32)
    kf = keys.astype(jnp.float32)
    vf = values.astype(jnp.float32)
    df = dmixed.astype(jnp.float32)
    scores = jnp.einsum('thd,shd->hts', qf, kf)
    local = jnp.where(mask[None], scores, 0.0).astype(jnp.bfloat16).astype(jnp.float32)
    dscore = jnp.einsum('the,she->hts', df, vf)
    dlocal = jnp.where(mask[None], dscore, 0.0).astype(jnp.bfloat16).astype(jnp.float32)
    grad_query = jnp.einsum('hts,shd->thd', dlocal, kf) + jnp.einsum('the,hde->thd', df, prior_bf)
    grad_key = jnp.einsum('hts,thd->shd', dlocal, qf) + jnp.einsum('she,hde->shd', vf, later_bf)
    grad_value = jnp.einsum('hts,the->she', local, df) + jnp.einsum('shd,hde->she', kf, later_bf)
    return (grad_query.astype(jnp.bfloat16), grad_key.astype(jnp.bfloat16), grad_value.astype(jnp.bfloat16))

def reference(query_rows, key_rows, value_rows, grad_rows):
    count = TOKENS // SPAN
    shape = (count, SPAN, HEADS, HEAD_DIM)
    query = query_rows.reshape(shape)
    keys = key_rows.reshape(shape)
    values = value_rows.reshape(shape)
    grads = grad_rows.reshape(shape)

    def forward_step(total, pair):
        kv_span = jnp.einsum('shd,she->hde', pair[0].astype(jnp.float32), pair[1].astype(jnp.float32))
        return (total + kv_span, total)
    zeros = jnp.zeros((HEADS, HEAD_DIM, HEAD_DIM), jnp.float32)
    unused, priors = lax.scan(forward_step, zeros, (keys, values))
    attended, dmixed, state_grads = lax.map(lambda item: span_front(*item), (query, keys, values, grads, priors))

    def backward_step(total, term):
        return (total + term, total)
    unused2, laters = lax.scan(backward_step, zeros, state_grads, reverse=True)
    grad_query, grad_key, grad_value = lax.map(lambda item: span_back(*item), (query, keys, values, dmixed, priors, laters))
    flat = (TOKENS, HEADS * HEAD_DIM)
    return (attended.reshape(flat), grad_query.reshape(flat), grad_key.reshape(flat), grad_value.reshape(flat))
```

```python
import functools

import jax
import jax.numpy as jnp
from jax import lax
from jax.experimental import pallas as pl
from jax.experimental.pallas import tpu as pltpu
from jax.sharding import Mesh, PartitionSpec as P

HEAD_DIM = 128
VMEM_LIMIT = 48 * 1024 * 1024
f32 = jnp.float32
bf16 = jnp.bfloat16


def dot_nn(a, b):
    return lax.dot_general(a, b, (((1,), (0,)), ((), ())), preferred_element_type=f32)


def dot_nt(a, b):
    return lax.dot_general(a, b, (((1,), (1,)), ((), ())), preferred_element_type=f32)


def dot_tn(a, b):
    return lax.dot_general(a, b, (((0,), (0,)), ((), ())), preferred_element_type=f32)


def call(kernel, out_shape, operands, flops=0, smem=()):
    in_specs = [
        pl.BlockSpec(memory_space=pltpu.SMEM if i in smem else pltpu.VMEM)
        for i in range(len(operands))
    ]
    outs = jax.tree.leaves(out_shape)
    moved = sum(x.size * x.dtype.itemsize for x in list(operands) + outs)
    return pl.pallas_call(
        kernel,
        out_shape=out_shape,
        in_specs=in_specs,
        out_specs=jax.tree.map(lambda _: pl.BlockSpec(memory_space=pltpu.VMEM), out_shape),
        compiler_params=pltpu.CompilerParams(vmem_limit_bytes=VMEM_LIMIT),
        cost_estimate=pl.CostEstimate(flops=flops, bytes_accessed=moved, transcendentals=0),
    )(*operands)


def head_slices(width):
    return [(h, slice(h * HEAD_DIM, (h + 1) * HEAD_DIM)) for h in range(width // HEAD_DIM)]


def causal(count):
    rows = lax.broadcasted_iota(jnp.int32, (count, count), 0)
    cols = lax.broadcasted_iota(jnp.int32, (count, count), 1)
    return rows >= cols


def state_kernel(k_ref, v_ref, out_ref):
    for h, cols in head_slices(k_ref.shape[1]):
        out_ref[h] = dot_tn(k_ref[:, cols], v_ref[:, cols]).astype(bf16)


def total_kernel(parts_ref, out_ref):
    total = parts_ref[0].astype(f32)
    for j in range(1, parts_ref.shape[0]):
        total = total + parts_ref[j].astype(f32)
    total = total.astype(bf16)
    for j in range(out_ref.shape[0]):
        out_ref[j] = total


def running_kernel(reverse, place_ref, parts_ref, totals_ref, out_ref):
    place = place_ref[0]
    acc = jnp.zeros(out_ref.shape[1:], f32)
    for z in range(totals_ref.shape[0]):
        wanted = z > place if reverse else z < place
        acc = acc + jnp.where(wanted, totals_ref[z].astype(f32), 0.0)
    order = range(parts_ref.shape[0])
    for j in reversed(order) if reverse else order:
        out_ref[j] = acc.astype(bf16)
        acc = acc + parts_ref[j].astype(f32)


def local_kernel(q_ref, k_ref, v_ref, local_ref, inner_ref):
    mask = causal(q_ref.shape[0])
    for h, cols in head_slices(q_ref.shape[1]):
        scores = dot_nt(q_ref[:, cols], k_ref[:, cols])
        local = jnp.where(mask, scores, 0.0).astype(bf16)
        local_ref[h] = local
        inner_ref[:, cols] = dot_nn(local, v_ref[:, cols])


def mixed_kernel(q_ref, g_ref, inner_ref, prior_ref, attended_ref, dy_ref, state_ref):
    for h, cols in head_slices(q_ref.shape[1]):
        query = q_ref[:, cols]
        mixed = inner_ref[:, cols] + dot_nn(query, prior_ref[h])
        scale = lax.rsqrt(jnp.mean(mixed * mixed, axis=-1, keepdims=True) + 1e-06)
        attended_ref[:, cols] = (mixed * scale).astype(bf16)
        grad = g_ref[:, cols].astype(f32)
        inner_mean = jnp.mean(grad * mixed, axis=-1, keepdims=True)
        dy = (scale * grad - mixed * (scale * scale * scale * inner_mean)).astype(bf16)
        dy_ref[:, cols] = dy
        state_ref[h] = dot_tn(query, dy).astype(bf16)


def side_kernel(q_ref, k_ref, v_ref, dy_ref, local_ref, prior_ref, gq_ref, gk_ref, gv_ref):
    mask = causal(q_ref.shape[0])
    for h, cols in head_slices(q_ref.shape[1]):
        dy = dy_ref[:, cols]
        dlocal = jnp.where(mask, dot_nt(dy, v_ref[:, cols]), 0.0).astype(bf16)
        gq_ref[:, cols] = (
            dot_nn(dlocal, k_ref[:, cols]) + dot_nt(dy, prior_ref[h])
        ).astype(bf16)
        gk_ref[:, cols] = dot_tn(dlocal, q_ref[:, cols])
        gv_ref[:, cols] = dot_tn(local_ref[h], dy)


def last_kernel(k_ref, v_ref, gk_ref, gv_ref, later_ref, out_k_ref, out_v_ref):
    for h, cols in head_slices(k_ref.shape[1]):
        later = later_ref[h]
        out_k_ref[:, cols] = (gk_ref[:, cols] + dot_nt(v_ref[:, cols], later)).astype(bf16)
        out_v_ref[:, cols] = (gv_ref[:, cols] + dot_nn(k_ref[:, cols], later)).astype(bf16)


def scan_states(states, reverse):
    heads, dim, _ = states.shape
    peers = lax.axis_size("plane")
    planes = lax.axis_size("z")
    rows = heads * dim // peers
    place = lax.axis_index("z").astype(jnp.int32).reshape(1)
    parts = lax.all_to_all(states.reshape(peers, rows, dim), "plane", 0, 0, tiled=True)
    sent = call(total_kernel, jax.ShapeDtypeStruct((planes, rows, dim), bf16), (parts,))
    totals = lax.all_to_all(sent, "z", 0, 0, tiled=True)
    running = call(
        functools.partial(running_kernel, reverse),
        jax.ShapeDtypeStruct((peers, rows, dim), bf16),
        (place, parts, totals),
        smem=(0,),
    )
    back = lax.all_to_all(running, "plane", 0, 0, tiled=True)
    return back.reshape(heads, dim, dim)


def per_device(query, keys, values, grads):
    tokens, width = query.shape
    heads = width // HEAD_DIM
    wide = jax.ShapeDtypeStruct((tokens, width), f32)
    narrow = jax.ShapeDtypeStruct((tokens, width), bf16)
    state = jax.ShapeDtypeStruct((heads, HEAD_DIM, HEAD_DIM), bf16)
    square = jax.ShapeDtypeStruct((heads, tokens, tokens), bf16)
    unit = 2 * tokens * width * HEAD_DIM
    kv = call(state_kernel, state, (keys, values), unit)
    prior = scan_states(kv, False)
    local, inner = call(local_kernel, (square, wide), (query, keys, values), 2 * unit)
    attended, dy, gq = call(
        mixed_kernel, (narrow, narrow, state), (query, grads, inner, prior), 2 * unit
    )
    later = scan_states(gq, True)
    grad_query, gk_side, gv_side = call(
        side_kernel, (narrow, wide, wide), (query, keys, values, dy, local, prior), 5 * unit
    )
    grad_key, grad_value = call(
        last_kernel, (narrow, narrow), (keys, values, gk_side, gv_side, later), 2 * unit
    )
    return attended, grad_query, grad_key, grad_value


def solution(mesh):
    planes = 16
    split = Mesh(mesh.devices.reshape(planes, -1), ("z", "plane"))
    placed = P(("z", "plane"), None)
    return jax.shard_map(
        per_device,
        mesh=split,
        in_specs=(placed,) * 4,
        out_specs=(placed,) * 4,
        check_vma=False,
    )
```

```python
import functools

import jax
import jax.numpy as jnp
from jax import lax
from jax.experimental import pallas as pl
from jax.experimental.pallas import tpu as pltpu
from jax.sharding import Mesh, PartitionSpec as P

HEAD_DIM = 128
VMEM_LIMIT = 16 * 1024 * 1024
f32 = jnp.float32
bf16 = jnp.bfloat16


def dot_nn(a, b):
    return lax.dot_general(a, b, (((1,), (0,)), ((), ())), preferred_element_type=f32)


def dot_nt(a, b):
    return lax.dot_general(a, b, (((1,), (1,)), ((), ())), preferred_element_type=f32)


def dot_tn(a, b):
    return lax.dot_general(a, b, (((0,), (0,)), ((), ())), preferred_element_type=f32)


def call(kernel, out_shape, operands, flops=0, smem=()):
    in_specs = [
        pl.BlockSpec(memory_space=pltpu.SMEM if i in smem else pltpu.VMEM)
        for i in range(len(operands))
    ]
    outs = jax.tree.leaves(out_shape)
    moved = sum(x.size * x.dtype.itemsize for x in list(operands) + outs)
    return pl.pallas_call(
        kernel,
        out_shape=out_shape,
        in_specs=in_specs,
        out_specs=jax.tree.map(lambda _: pl.BlockSpec(memory_space=pltpu.VMEM), out_shape),
        compiler_params=pltpu.CompilerParams(vmem_limit_bytes=VMEM_LIMIT),
        cost_estimate=pl.CostEstimate(flops=flops, bytes_accessed=moved, transcendentals=0),
    )(*operands)


def head_slices(width):
    return [(h, slice(h * HEAD_DIM, (h + 1) * HEAD_DIM)) for h in range(width // HEAD_DIM)]


def causal(count):
    rows = lax.broadcasted_iota(jnp.int32, (count, count), 0)
    cols = lax.broadcasted_iota(jnp.int32, (count, count), 1)
    return rows >= cols


def state_kernel(k_ref, v_ref, out_ref):
    for h, cols in head_slices(k_ref.shape[1]):
        out_ref[h] = dot_tn(k_ref[:, cols], v_ref[:, cols]).astype(bf16)


def total_kernel(parts_ref, out_ref):
    total = parts_ref[0].astype(f32)
    for j in range(1, parts_ref.shape[0]):
        total = total + parts_ref[j].astype(f32)
    total = total.astype(bf16)
    for j in range(out_ref.shape[0]):
        out_ref[j] = total


def running_kernel(reverse, place_ref, parts_ref, totals_ref, out_ref):
    place = place_ref[0]
    acc = jnp.zeros(out_ref.shape[1:], f32)
    for b in range(totals_ref.shape[0]):
        wanted = b > place if reverse else b < place
        acc = acc + jnp.where(wanted, totals_ref[b].astype(f32), 0.0)
    order = range(parts_ref.shape[0])
    for j in reversed(order) if reverse else order:
        out_ref[j] = acc.astype(bf16)
        acc = acc + parts_ref[j].astype(f32)


def local_kernel(q_ref, k_ref, v_ref, local_ref, inner_ref):
    mask = causal(q_ref.shape[0])
    for h, cols in head_slices(q_ref.shape[1]):
        scores = dot_nt(q_ref[:, cols], k_ref[:, cols])
        local = jnp.where(mask, scores, 0.0).astype(bf16)
        local_ref[h] = local
        inner_ref[:, cols] = dot_nn(local, v_ref[:, cols])


def mixed_kernel(q_ref, g_ref, inner_ref, prior_ref, normed_ref, dy_ref, state_ref):
    for h, cols in head_slices(q_ref.shape[1]):
        query = q_ref[:, cols]
        mixed = inner_ref[:, cols] + dot_nn(query, prior_ref[h])
        scale = lax.rsqrt(jnp.mean(mixed * mixed, axis=-1, keepdims=True) + 1e-06)
        normed_ref[:, cols] = (mixed * scale).astype(bf16)
        grad = g_ref[:, cols].astype(f32)
        inner_mean = jnp.mean(grad * mixed, axis=-1, keepdims=True)
        dy = (scale * grad - mixed * (scale * scale * scale * inner_mean)).astype(bf16)
        dy_ref[:, cols] = dy
        state_ref[h] = dot_tn(query, dy).astype(bf16)


def side_kernel(
    q_ref, k_ref, v_ref, dy_ref, local_ref, prior_ref, normed_ref, gq_ref, gk_ref, gv_ref, attended_ref
):
    attended_ref[...] = normed_ref[...]
    mask = causal(q_ref.shape[0])
    for h, cols in head_slices(q_ref.shape[1]):
        dy = dy_ref[:, cols]
        dlocal = jnp.where(mask, dot_nt(dy, v_ref[:, cols]), 0.0).astype(bf16)
        gq_ref[:, cols] = (
            dot_nn(dlocal, k_ref[:, cols]) + dot_nt(dy, prior_ref[h])
        ).astype(bf16)
        gk_ref[:, cols] = dot_tn(dlocal, q_ref[:, cols])
        gv_ref[:, cols] = dot_tn(local_ref[h], dy)


def last_kernel(k_ref, v_ref, gk_ref, gv_ref, later_ref, out_k_ref, out_v_ref):
    for h, cols in head_slices(k_ref.shape[1]):
        later = later_ref[h]
        out_k_ref[:, cols] = (gk_ref[:, cols] + dot_nt(v_ref[:, cols], later)).astype(bf16)
        out_v_ref[:, cols] = (gv_ref[:, cols] + dot_nn(k_ref[:, cols], later)).astype(bf16)


def scan_states(states, reverse):
    heads, dim, _ = states.shape
    peers = lax.axis_size("inner")
    blocks = lax.axis_size("outer")
    rows = heads * dim // peers
    place = lax.axis_index("outer").astype(jnp.int32).reshape(1)
    parts = lax.all_to_all(states.reshape(peers, rows, dim), "inner", 0, 0, tiled=True)
    sent = call(total_kernel, jax.ShapeDtypeStruct((blocks, rows, dim), bf16), (parts,))
    totals = lax.all_to_all(sent, "outer", 0, 0, tiled=True)
    running = call(
        functools.partial(running_kernel, reverse),
        jax.ShapeDtypeStruct((peers, rows, dim), bf16),
        (place, parts, totals),
        smem=(0,),
    )
    back = lax.all_to_all(running, "inner", 0, 0, tiled=True)
    return back.reshape(heads, dim, dim)


def per_device(query, keys, values, grads):
    tokens, width = query.shape
    heads = width // HEAD_DIM
    wide = jax.ShapeDtypeStruct((tokens, width), f32)
    narrow = jax.ShapeDtypeStruct((tokens, width), bf16)
    state = jax.ShapeDtypeStruct((heads, HEAD_DIM, HEAD_DIM), bf16)
    square = jax.ShapeDtypeStruct((heads, tokens, tokens), bf16)
    unit = 2 * tokens * width * HEAD_DIM
    kv = call(state_kernel, state, (keys, values), unit)
    prior = scan_states(kv, False)
    local, inner = call(local_kernel, (square, wide), (query, keys, values), 2 * unit)
    normed, dy, gq = call(
        mixed_kernel, (narrow, narrow, state), (query, grads, inner, prior), 2 * unit
    )
    later = scan_states(gq, True)
    grad_query, gk_side, gv_side, attended = call(
        side_kernel,
        (narrow, wide, wide, narrow),
        (query, keys, values, dy, local, prior, normed),
        5 * unit,
    )
    grad_key, grad_value = call(
        last_kernel, (narrow, narrow), (keys, values, gk_side, gv_side, later), 2 * unit
    )
    return attended, grad_query, grad_key, grad_value


def solution(mesh):
    split = Mesh(mesh.devices.reshape(-1, 64), ("outer", "inner"))
    placed = P(("outer", "inner"), None)
    return jax.shard_map(
        per_device,
        mesh=split,
        in_specs=(placed,) * 4,
        out_specs=(placed,) * 4,
        check_vma=False,
    )
```

```python
import functools

import jax
import jax.numpy as jnp
from jax import lax
from jax.experimental import pallas as pl
from jax.experimental.pallas import tpu as pltpu
from jax.sharding import Mesh, PartitionSpec as P

HEAD_DIM = 128
GROUP = 512
MIB = 1024 * 1024
LARGE = 56 * MIB
STATE_LIMIT = 53 * MIB
MIXED_LIMIT = 52 * MIB
LAST_LIMIT = 52 * MIB
SMALL = 16 * MIB
f32 = jnp.float32
bf16 = jnp.bfloat16


def dot_nn(a, b):
    return lax.dot_general(a, b, (((1,), (0,)), ((), ())), preferred_element_type=f32)


def dot_nt(a, b):
    return lax.dot_general(a, b, (((1,), (1,)), ((), ())), preferred_element_type=f32)


def dot_tn(a, b):
    return lax.dot_general(a, b, (((0,), (0,)), ((), ())), preferred_element_type=f32)


def shape(*dims, dtype=bf16):
    return jax.ShapeDtypeStruct(dims, dtype)


def call(kernel, out_shape, operands, limit, flops=0, far=(), far_out=(), smem=(), scratch=()):
    def space(i, kept):
        return pl.BlockSpec(memory_space=pltpu.HBM if i in kept else pltpu.VMEM)

    in_specs = [
        pl.BlockSpec(memory_space=pltpu.SMEM) if i in smem else space(i, far)
        for i in range(len(operands))
    ]
    out_specs = tuple(space(i, far_out) for i in range(len(out_shape)))
    moved = sum(x.size * x.dtype.itemsize for x in tuple(operands) + out_shape)
    return pl.pallas_call(
        kernel,
        out_shape=out_shape,
        in_specs=in_specs,
        out_specs=out_specs,
        scratch_shapes=scratch,
        compiler_params=pltpu.CompilerParams(vmem_limit_bytes=limit),
        cost_estimate=pl.CostEstimate(flops=flops, bytes_accessed=moved, transcendentals=0),
    )(*operands)


def copies_of(pairs, sems, first=0):
    return [
        pltpu.make_async_copy(src, dst, sems.at[first + i]) for i, (src, dst) in enumerate(pairs)
    ]


def start_all(copies):
    for copy in copies:
        copy.start()


def wait_all(copies):
    for copy in copies:
        copy.wait()


def cut(ref, g):
    return ref.at[:, pl.ds(g * GROUP, GROUP)]


def grouped(pairs, sems):
    count = pairs[0][0].shape[1] // GROUP
    return [
        copies_of([(cut(src, g), cut(dst, g)) for src, dst in pairs], sems, g * len(pairs))
        for g in range(count)
    ]


def group_heads(g):
    heads = range(g * GROUP // HEAD_DIM, (g + 1) * GROUP // HEAD_DIM)
    return [(h, slice(h * HEAD_DIM, (h + 1) * HEAD_DIM)) for h in heads]


def half(ref, which):
    count = ref.shape[-1] // 2
    return ref.at[:, pl.ds(pl.multiple_of(which * count, count), count)]


def causal(count):
    rows = lax.broadcasted_iota(jnp.int32, (count, count), 0)
    cols = lax.broadcasted_iota(jnp.int32, (count, count), 1)
    return rows >= cols


def state_kernel(k_far, v_far, out_ref, k_ref, v_ref, sems):
    pairs, rows, _ = out_ref.shape
    cuts = HEAD_DIM // rows
    heads = pairs // cuts // 2
    copies = grouped([(k_far, k_ref), (v_far, v_ref)], sems)
    for group in copies:
        start_all(group)
    for g, group in enumerate(copies):
        wait_all(group)
        for h, cols in group_heads(g):
            state = dot_tn(k_ref[:, cols], v_ref[:, cols]).astype(bf16)
            for q in range(cuts):
                place = 2 * ((h % heads) * cuts + q) + h // heads
                out_ref[place] = state[q * rows : (q + 1) * rows]


def total_kernel(parts_ref, *refs):
    out_ref = refs[-1]
    total = parts_ref[0].astype(f32)
    for j in range(1, parts_ref.shape[0]):
        total = total + parts_ref[j].astype(f32)
    total = total.astype(bf16)
    for j in range(out_ref.shape[0]):
        out_ref[j] = total


def outer_sum(reverse, place, totals_ref):
    acc = jnp.zeros(totals_ref.shape[1:], f32)
    for b in range(totals_ref.shape[0]):
        wanted = b > place if reverse else b < place
        acc = acc + jnp.where(wanted, totals_ref[b].astype(f32), 0.0)
    return acc


def prior_kernel(place_ref, parts_ref, totals_ref, token_ref, out_ref):
    acc = outer_sum(False, place_ref[0], totals_ref)
    for r in range(out_ref.shape[0]):
        out_ref[r] = acc.astype(bf16)
        acc = acc + parts_ref[2 * r].astype(f32) + parts_ref[2 * r + 1].astype(f32)


def later_kernel(place_ref, parts_ref, totals_ref, token_ref, out_ref):
    acc = outer_sum(True, place_ref[0], totals_ref)
    for r in reversed(range(parts_ref.shape[0])):
        out_ref[2 * r] = acc.astype(bf16)
        out_ref[2 * r + 1] = acc.astype(bf16)
        acc = acc + parts_ref[r].astype(f32)


def pack_kernel(core_ref, q_far, k_far, v_far, g_far, out_ref, token_ref, sems):
    other = 1 - core_ref[0]
    rows = (q_far, k_far, v_far, g_far)
    copies = copies_of([(half(src, other), out_ref.at[i]) for i, src in enumerate(rows)], sems)
    start_all(copies)
    token_ref[...] = jnp.zeros_like(token_ref)
    wait_all(copies)


def local_kernel(
    core_ref, q_far, k_far, v_far, g_far, recv_far,
    inner_ref, qg_ref, kv_ref, token_ref, sems,
):
    core = core_ref[0]
    count = q_far.shape[0]
    mine = pl.ds(pl.multiple_of(core * count, count), count)
    theirs = pl.ds(pl.multiple_of((1 - core) * count, count), count)
    q_ref, k_ref, v_ref = qg_ref.at[0], kv_ref.at[0], kv_ref.at[1]
    near = (q_ref, k_ref, v_ref, qg_ref.at[1])
    copies = copies_of(
        [(half(src, core), dst.at[mine]) for src, dst in zip((q_far, k_far, v_far, g_far), near)]
        + [(recv_far.at[i], dst.at[theirs]) for i, dst in enumerate(near)],
        sems,
    )
    start_all(copies)
    token_ref[...] = jnp.zeros_like(token_ref)
    wait_all(copies)
    mask = causal(2 * count)
    for g in range(q_ref.shape[1] // GROUP):
        for h, cols in group_heads(g):
            scores = dot_nt(q_ref[:, cols], k_ref[:, cols])
            local = jnp.where(mask, scores, 0.0).astype(bf16)
            inner_ref[:, cols] = dot_nn(local, v_ref[:, cols])


def whole_state(ref, h):
    cuts = HEAD_DIM // ref.shape[1]
    return jnp.concatenate([ref[h * cuts + q] for q in range(cuts)], axis=0)


def normed_parts(mixed, grad):
    scale = lax.rsqrt(jnp.mean(mixed * mixed, axis=-1, keepdims=True) + 1e-06)
    inner_mean = jnp.mean(grad * mixed, axis=-1, keepdims=True)
    dy = (scale * grad - mixed * (scale * scale * scale * inner_mean)).astype(bf16)
    return scale, dy


def mixed_kernel(qg_far, inner_ref, prior_ref, state_ref, qg_ref, sems):
    rows = state_ref.shape[1]
    cuts = HEAD_DIM // rows
    q_ref, g_ref = qg_ref.at[0], qg_ref.at[1]
    copies = grouped([(qg_far.at[i], qg_ref.at[i]) for i in range(2)], sems)
    for group in copies:
        start_all(group)
    for g, group in enumerate(copies):
        wait_all(group)
        for h, cols in group_heads(g):
            query = q_ref[:, cols]
            mixed = inner_ref[:, cols] + dot_nn(query, whole_state(prior_ref, h))
            _, dy = normed_parts(mixed, g_ref[:, cols].astype(f32))
            state = dot_tn(query, dy).astype(bf16)
            for q in range(cuts):
                state_ref[h * cuts + q] = state[q * rows : (q + 1) * rows]


def side_kernel(
    core_ref, qg_far, kv_far, inner_far, prior_far, own_ref, send_ref, token_ref,
    qg_ref, kv_ref, inner_ref, prior_ref, tile_ref, sems, prior_sem,
):
    core = core_ref[0]
    count = own_ref.shape[1]
    q_ref, g_ref, k_ref, v_ref = qg_ref.at[0], qg_ref.at[1], kv_ref.at[0], kv_ref.at[1]
    copies = grouped(
        [(qg_far.at[i], qg_ref.at[i]) for i in range(2)]
        + [(kv_far.at[i], kv_ref.at[i]) for i in range(2)]
        + [(inner_far, inner_ref)],
        sems,
    )
    prior_copy = copies_of([(prior_far, prior_ref)], prior_sem)
    start_all(prior_copy)
    for group in copies:
        start_all(group)
    token_ref[...] = jnp.zeros_like(token_ref)
    mask = causal(2 * count)
    wait_all(prior_copy)
    for g, group in enumerate(copies):
        wait_all(group)
        for h, cols in group_heads(g):
            query, key, value = q_ref[:, cols], k_ref[:, cols], v_ref[:, cols]
            prior = whole_state(prior_ref, h)
            local = jnp.where(mask, dot_nt(query, key), 0.0).astype(bf16)
            mixed = inner_ref[:, cols] + dot_nn(query, prior)
            scale, dy = normed_parts(mixed, g_ref[:, cols].astype(f32))
            dlocal = jnp.where(mask, dot_nt(dy, value), 0.0).astype(bf16)
            tile_ref[0, :, cols] = (mixed * scale).astype(bf16)
            tile_ref[1, :, cols] = (dot_nn(dlocal, key) + dot_nt(dy, prior)).astype(bf16)
            tile_ref[2, :, cols] = dot_tn(dlocal, query).astype(bf16)
            tile_ref[3, :, cols] = dot_tn(local, dy).astype(bf16)
    mine = pl.ds(pl.multiple_of(core * count, count), count)
    theirs = pl.ds(pl.multiple_of((1 - core) * count, count), count)
    for i in range(own_ref.shape[0]):
        own_ref[i] = tile_ref[i, mine]
        send_ref[i] = tile_ref[i, theirs]


def finish_kernel(core_ref, own_far, recv_far, attended_ref, gq_ref, side_ref, sems):
    core = core_ref[0]
    outs = (attended_ref, gq_ref, side_ref.at[0], side_ref.at[1])
    copies = copies_of(
        [(own_far.at[i], half(dst, core)) for i, dst in enumerate(outs)]
        + [(recv_far.at[i], half(dst, 1 - core)) for i, dst in enumerate(outs)],
        sems,
    )
    start_all(copies)
    wait_all(copies)


def last_kernel(
    k_ref, v_ref, side_far, later_ref, out_k_far, out_v_far,
    side_ref, out_k_ref, out_v_ref, sems, out_sems,
):
    cuts = HEAD_DIM // later_ref.shape[1]
    heads = later_ref.shape[0] // cuts // 2
    copies = grouped([(side_far.at[i], side_ref.at[i]) for i in range(2)], sems)
    out_copies = grouped([(out_k_ref, out_k_far), (out_v_ref, out_v_far)], out_sems)
    for group in copies:
        start_all(group)
    for g, group in enumerate(out_copies):
        wait_all(copies[g])
        for h, cols in group_heads(g):
            places = [2 * ((h % heads) * cuts + q) + h // heads for q in range(cuts)]
            later = jnp.concatenate([later_ref[i] for i in places], axis=0)
            gk = side_ref[0, :, cols].astype(f32) + dot_nt(v_ref[:, cols], later)
            gv = side_ref[1, :, cols].astype(f32) + dot_nn(k_ref[:, cols], later)
            out_k_ref[:, cols] = gk.astype(bf16)
            out_v_ref[:, cols] = gv.astype(bf16)
        start_all(group)
    for group in out_copies:
        wait_all(group)


def per_device(query, keys, values, grads):
    tokens, width = query.shape
    part = width // 2
    pairs = lax.axis_size("pair")
    blocks = lax.axis_size("outer")
    both = ("pair", "core")
    slice_rows = part // pairs
    groups = width // GROUP
    part_groups = part // GROUP
    unit = 2 * tokens * width * HEAD_DIM
    core = lax.axis_index("core").astype(jnp.int32).reshape(1)
    place = lax.axis_index("outer").astype(jnp.int32).reshape(1)
    swap = [(0, 1), (1, 0)]

    def vmem(*dims, dtype=bf16):
        return pltpu.VMEM(dims, dtype)

    def sems(count):
        return pltpu.SemaphoreType.DMA((count,))

    pair_rows = vmem(2, 2 * tokens, part)
    pair_rows_f32 = vmem(2 * tokens, part, dtype=f32)
    rows = vmem(tokens, width)
    totals_shape = (shape(blocks, slice_rows, HEAD_DIM),)
    half_states = shape(pairs, slice_rows, HEAD_DIM)
    states = shape(2 * pairs, slice_rows, HEAD_DIM)
    pair_tiles = shape(2, 2 * tokens, part)

    out = shape(tokens, width)
    token = shape(8, 128, dtype=f32)
    (kv,) = call(
        state_kernel, (states,), (keys, values), STATE_LIMIT, unit,
        far=(0, 1), scratch=(rows, rows, sems(2 * groups)),
    )
    kv_parts = lax.all_to_all(kv, both, 0, 0, tiled=True)
    send, packed = call(
        pack_kernel, (shape(4, tokens, part), token), (core, query, keys, values, grads), LARGE,
        far=(1, 2, 3, 4), smem=(0,), scratch=(sems(4),),
    )
    recv = lax.ppermute(send, "core", swap)
    (sent,) = call(total_kernel, totals_shape, (kv_parts, packed), SMALL, far=(1,))
    kv_totals = lax.all_to_all(sent, "outer", 0, 0, tiled=True)
    inner, qg, kv_pair, ready = call(
        local_kernel,
        (shape(2 * tokens, part, dtype=f32), pair_tiles, pair_tiles, token),
        (core, query, keys, values, grads, recv),
        LARGE, 4 * unit,
        far=(1, 2, 3, 4, 5), smem=(0,), scratch=(sems(8),),
    )
    (running,) = call(
        prior_kernel, (half_states,), (place, kv_parts, kv_totals, ready), SMALL,
        far=(3,), smem=(0,),
    )
    prior = lax.all_to_all(running, "pair", 0, 0, tiled=True)
    (gq_state,) = call(
        mixed_kernel, (half_states,), (qg, inner, prior), MIXED_LIMIT, 2 * unit,
        far=(0,), scratch=(pair_rows, sems(2 * part_groups)),
    )
    gq_parts = lax.all_to_all(gq_state, "pair", 0, 0, tiled=True)
    own, send, done = call(
        side_kernel, (shape(4, tokens, part), shape(4, tokens, part), token),
        (core, qg, kv_pair, inner, prior), LARGE, 10 * unit,
        far=(1, 2, 3, 4), smem=(0,),
        scratch=(
            pair_rows, pair_rows, pair_rows_f32, vmem(pairs, slice_rows, HEAD_DIM), vmem(4, 2 * tokens, part),
            sems(5 * part_groups), sems(1),
        ),
    )
    (sent,) = call(total_kernel, totals_shape, (gq_parts,), SMALL)
    gq_totals = lax.all_to_all(sent, "outer", 0, 0, tiled=True)
    recv = lax.ppermute(send, "core", swap)
    attended, grad_query, sides = call(
        finish_kernel, (out, out, shape(2, tokens, width)), (core, own, recv), LARGE,
        far=(1, 2), smem=(0,), scratch=(sems(8),),
    )
    (running,) = call(
        later_kernel, (states,), (place, gq_parts, gq_totals, done), SMALL,
        far=(3,), smem=(0,),
    )
    later = lax.all_to_all(running, both, 0, 0, tiled=True)
    grad_key, grad_value = call(
        last_kernel, (out, out), (keys, values, sides, later), LAST_LIMIT, 2 * unit,
        far=(2,), far_out=(0, 1),
        scratch=(vmem(2, tokens, width), rows, rows, sems(2 * groups), sems(2 * groups)),
    )
    return attended, grad_query, grad_key, grad_value


def solution(mesh):
    split = Mesh(mesh.devices.reshape(-1, 32, 2), ("outer", "pair", "core"))
    placed = P(("outer", "pair", "core"), None)
    return jax.shard_map(
        per_device,
        mesh=split,
        in_specs=(placed,) * 4,
        out_specs=(placed,) * 4,
        check_vma=False,
    )
```

```python
import functools

import jax
import jax.numpy as jnp
from jax import lax
from jax.experimental import pallas as pl
from jax.experimental.pallas import tpu as pltpu
from jax.sharding import Mesh, PartitionSpec as P

HEAD_DIM = 128
GROUP = 512
MIB = 1024 * 1024
LIMITS = {
    "total": 53 * MIB,
    "prior": 53 * MIB,
    "later": 53 * MIB,
    "mixed": 51 * MIB,
    "finish": 48 * MIB,
    "last": 50 * MIB,
    "local": 56 * MIB,
    "side": 56 * MIB,
    "state": 53 * MIB,
    "pack": 56 * MIB,
}
f32 = jnp.float32
bf16 = jnp.bfloat16
OUTER_TURN = 4
INNER_TURN = 20
PAIR_TURN = INNER_TURN // 2


def dot_nn(a, b):
    return lax.dot_general(a, b, (((1,), (0,)), ((), ())), preferred_element_type=f32)


def dot_nt(a, b):
    return lax.dot_general(a, b, (((1,), (1,)), ((), ())), preferred_element_type=f32)


def dot_tn(a, b):
    return lax.dot_general(a, b, (((0,), (0,)), ((), ())), preferred_element_type=f32)


def shape(*dims, dtype=bf16):
    return jax.ShapeDtypeStruct(dims, dtype)


def call(kernel, out_shape, operands, limit, flops=0, far=(), far_out=(), smem=(), scratch=()):
    def space(i, kept):
        return pl.BlockSpec(memory_space=pltpu.HBM if i in kept else pltpu.VMEM)

    in_specs = [
        pl.BlockSpec(memory_space=pltpu.SMEM) if i in smem else space(i, far)
        for i in range(len(operands))
    ]
    out_specs = tuple(space(i, far_out) for i in range(len(out_shape)))
    moved = sum(x.size * x.dtype.itemsize for x in tuple(operands) + out_shape)
    return pl.pallas_call(
        kernel,
        out_shape=out_shape,
        in_specs=in_specs,
        out_specs=out_specs,
        scratch_shapes=scratch,
        compiler_params=pltpu.CompilerParams(vmem_limit_bytes=limit),
        cost_estimate=pl.CostEstimate(flops=flops, bytes_accessed=moved, transcendentals=0),
    )(*operands)


def copies_of(pairs, sems, first=0):
    return [
        pltpu.make_async_copy(src, dst, sems.at[first + i]) for i, (src, dst) in enumerate(pairs)
    ]


def start_all(copies):
    for copy in copies:
        copy.start()


def wait_all(copies):
    for copy in copies:
        copy.wait()


def cut(ref, g):
    return ref.at[:, pl.ds(g * GROUP, GROUP)]


def grouped(pairs, sems):
    count = pairs[0][0].shape[1] // GROUP
    return [
        copies_of([(cut(src, g), cut(dst, g)) for src, dst in pairs], sems, g * len(pairs))
        for g in range(count)
    ]


def group_heads(g):
    heads = range(g * GROUP // HEAD_DIM, (g + 1) * GROUP // HEAD_DIM)
    return [(h, slice(h * HEAD_DIM, (h + 1) * HEAD_DIM)) for h in heads]


def half(ref, which):
    count = ref.shape[-1] // 2
    return ref.at[:, pl.ds(pl.multiple_of(which * count, count), count)]


def causal(count):
    rows = lax.broadcasted_iota(jnp.int32, (count, count), 0)
    cols = lax.broadcasted_iota(jnp.int32, (count, count), 1)
    return rows >= cols


def state_kernel(k_far, v_far, out_ref, k_ref, v_ref, sems):
    pairs, rows, _ = out_ref.shape
    cuts = HEAD_DIM // rows
    heads = pairs // cuts // 2
    copies = grouped([(k_far, k_ref), (v_far, v_ref)], sems)
    for group in copies:
        start_all(group)
    for g, group in enumerate(copies):
        wait_all(group)
        for h, cols in group_heads(g):
            state = dot_tn(k_ref[:, cols], v_ref[:, cols]).astype(bf16)
            for q in range(cuts):
                place = 2 * ((h % heads) * cuts + q) + h // heads
                out_ref[place ^ INNER_TURN] = state[q * rows : (q + 1) * rows]


def total_kernel(parts_ref, *refs):
    out_ref = refs[-1]
    total = parts_ref[0].astype(f32)
    for j in range(1, parts_ref.shape[0]):
        total = total + parts_ref[j].astype(f32)
    total = total.astype(bf16)
    for j in range(out_ref.shape[0]):
        out_ref[j] = total


def outer_sum(reverse, place, totals_ref):
    acc = jnp.zeros(totals_ref.shape[1:], f32)
    for b in range(totals_ref.shape[0]):
        wanted = b > place if reverse else b < place
        acc = acc + jnp.where(wanted, totals_ref[b ^ OUTER_TURN].astype(f32), 0.0)
    return acc


def prior_kernel(place_ref, parts_ref, totals_ref, after_ref, out_ref):
    acc = outer_sum(False, place_ref[0], totals_ref)
    for r in range(out_ref.shape[0]):
        out_ref[r ^ PAIR_TURN] = acc.astype(bf16)
        for i in (2 * r, 2 * r + 1):
            acc = acc + parts_ref[i ^ INNER_TURN].astype(f32)


def later_kernel(place_ref, parts_ref, totals_ref, after_ref, out_ref):
    acc = outer_sum(True, place_ref[0], totals_ref)
    for r in reversed(range(parts_ref.shape[0])):
        for i in (2 * r, 2 * r + 1):
            out_ref[i ^ INNER_TURN] = acc.astype(bf16)
        acc = acc + parts_ref[r ^ PAIR_TURN].astype(f32)


def pack_kernel(core_ref, q_far, k_far, v_far, g_far, out_ref, sems):
    other = 1 - core_ref[0]
    rows = (q_far, k_far, v_far, g_far)
    copies = copies_of([(half(src, other), out_ref.at[i]) for i, src in enumerate(rows)], sems)
    start_all(copies)
    wait_all(copies)


def local_kernel(
    core_ref, q_far, k_far, v_far, g_far, recv_far,
    inner_ref, qg_ref, kv_ref, sems,
):
    core = core_ref[0]
    count = q_far.shape[0]
    mine = pl.ds(pl.multiple_of(core * count, count), count)
    theirs = pl.ds(pl.multiple_of((1 - core) * count, count), count)
    q_ref, k_ref, v_ref = qg_ref.at[0], kv_ref.at[0], kv_ref.at[1]
    near = (q_ref, k_ref, v_ref, qg_ref.at[1])
    copies = copies_of(
        [(half(src, core), dst.at[mine]) for src, dst in zip((q_far, k_far, v_far, g_far), near)]
        + [(recv_far.at[i], dst.at[theirs]) for i, dst in enumerate(near)],
        sems,
    )
    start_all(copies)
    wait_all(copies)
    mask = causal(2 * count)
    for g in range(q_ref.shape[1] // GROUP):
        for h, cols in group_heads(g):
            scores = dot_nt(q_ref[:, cols], k_ref[:, cols])
            local = jnp.where(mask, scores, 0.0).astype(bf16)
            inner_ref[:, cols] = dot_nn(local, v_ref[:, cols])


def whole_state(ref, h):
    cuts = HEAD_DIM // ref.shape[1]
    return jnp.concatenate([ref[(h * cuts + q) ^ PAIR_TURN] for q in range(cuts)], axis=0)


def normed_parts(mixed, grad):
    scale = lax.rsqrt(jnp.mean(mixed * mixed, axis=-1, keepdims=True) + 1e-06)
    inner_mean = jnp.mean(grad * mixed, axis=-1, keepdims=True)
    dy = (scale * grad - mixed * (scale * scale * scale * inner_mean)).astype(bf16)
    return scale, dy


def mixed_kernel(qg_ref, inner_far, prior_ref, state_ref, inner_ref, sems):
    rows = state_ref.shape[1]
    cuts = HEAD_DIM // rows
    q_ref, g_ref = qg_ref.at[0], qg_ref.at[1]
    copies = grouped([(inner_far, inner_ref)], sems)
    for group in copies:
        start_all(group)
    for g, group in enumerate(copies):
        wait_all(group)
        for h, cols in group_heads(g):
            query = q_ref[:, cols]
            mixed = inner_ref[:, cols] + dot_nn(query, whole_state(prior_ref, h))
            _, dy = normed_parts(mixed, g_ref[:, cols].astype(f32))
            state = dot_tn(query, dy).astype(bf16)
            for q in range(cuts):
                state_ref[(h * cuts + q) ^ PAIR_TURN] = state[q * rows : (q + 1) * rows]


def side_kernel(
    first, core_ref, qg_far, kv_far, inner_far, prior_far, own_ref, send_ref,
    qg_ref, kv_ref, inner_ref, prior_ref, tile_ref, sems, prior_sem,
):
    core = core_ref[0]
    count = own_ref.shape[1]
    q_ref, g_ref, k_ref, v_ref = qg_ref.at[0], qg_ref.at[1], kv_ref.at[0], kv_ref.at[1]
    mine_cols = pl.ds(first * HEAD_DIM, inner_ref.shape[1])
    copies = grouped(
        [(qg_far.at[i, :, mine_cols], qg_ref.at[i]) for i in range(2)]
        + [(kv_far.at[i, :, mine_cols], kv_ref.at[i]) for i in range(2)]
        + [(inner_far.at[:, mine_cols], inner_ref)],
        sems,
    )
    prior_copy = copies_of([(prior_far, prior_ref)], prior_sem)
    start_all(prior_copy)
    for group in copies:
        start_all(group)
    mask = causal(2 * count)
    wait_all(prior_copy)
    for g, group in enumerate(copies):
        wait_all(group)
        for h, cols in group_heads(g):
            query, key, value = q_ref[:, cols], k_ref[:, cols], v_ref[:, cols]
            prior = whole_state(prior_ref, first + h)
            local = jnp.where(mask, dot_nt(query, key), 0.0).astype(bf16)
            mixed = inner_ref[:, cols] + dot_nn(query, prior)
            scale, dy = normed_parts(mixed, g_ref[:, cols].astype(f32))
            dlocal = jnp.where(mask, dot_nt(dy, value), 0.0).astype(bf16)
            tile_ref[0, :, cols] = (mixed * scale).astype(bf16)
            tile_ref[1, :, cols] = (dot_nn(dlocal, key) + dot_nt(dy, prior)).astype(bf16)
            tile_ref[2, :, cols] = dot_tn(dlocal, query).astype(bf16)
            tile_ref[3, :, cols] = dot_tn(local, dy).astype(bf16)
    mine = pl.ds(pl.multiple_of(core * count, count), count)
    theirs = pl.ds(pl.multiple_of((1 - core) * count, count), count)
    for i in range(own_ref.shape[0]):
        own_ref[i] = tile_ref[i, mine]
        send_ref[i] = tile_ref[i, theirs]


def swapped_copies(core, first, outs, own_a, own_b, recv_a, recv_b, sems):
    pairs = []
    for j, (own, recv) in enumerate(((own_a, recv_a), (own_b, recv_b))):
        for i, dst in enumerate(outs):
            quarter = dst.shape[1] // 4
            for src, which in ((own, core), (recv, 1 - core)):
                start = pl.multiple_of((2 * which + j) * quarter, quarter)
                pairs.append((src.at[first + i], dst.at[:, pl.ds(start, quarter)]))
    return copies_of(pairs, sems)


def finish_kernel(core_ref, own_a, own_b, recv_a, recv_b, attended_ref, gq_ref, sems):
    outs = (attended_ref, gq_ref)
    copies = swapped_copies(core_ref[0], 0, outs, own_a, own_b, recv_a, recv_b, sems)
    start_all(copies)
    wait_all(copies)


def last_kernel(
    core_ref, k_ref, v_ref, own_a, own_b, recv_a, recv_b, later_ref, out_k_far, out_v_far,
    gk_ref, gv_ref, out_k_ref, out_v_ref, sems, out_sems,
):
    cuts = HEAD_DIM // later_ref.shape[1]
    heads = later_ref.shape[0] // cuts // 2
    sides = (gk_ref, gv_ref)
    copies = swapped_copies(core_ref[0], 2, sides, own_a, own_b, recv_a, recv_b, sems)
    out_copies = grouped([(out_k_ref, out_k_far), (out_v_ref, out_v_far)], out_sems)
    start_all(copies)
    wait_all(copies)
    for g, group in enumerate(out_copies):
        for h, cols in group_heads(g):
            places = [2 * ((h % heads) * cuts + q) + h // heads for q in range(cuts)]
            later = jnp.concatenate([later_ref[i ^ INNER_TURN] for i in places], axis=0)
            gk = gk_ref[:, cols].astype(f32) + dot_nt(v_ref[:, cols], later)
            gv = gv_ref[:, cols].astype(f32) + dot_nn(k_ref[:, cols], later)
            out_k_ref[:, cols] = gk.astype(bf16)
            out_v_ref[:, cols] = gv.astype(bf16)
        start_all(group)
    for group in out_copies:
        wait_all(group)


def exchange(blocks, axis, groups):
    return lax.all_to_all(blocks, axis, 0, 0, tiled=True, axis_index_groups=groups)


def per_device(query, keys, values, grads):
    tokens, width = query.shape
    part = width // 2
    pairs = lax.axis_size("inner") // 2
    blocks = lax.axis_size("outer")
    slice_rows = part // pairs
    groups = width // GROUP
    part_groups = part // GROUP
    unit = 2 * tokens * width * HEAD_DIM
    core = (lax.axis_index("inner").astype(jnp.int32) % 2).reshape(1)
    place = lax.axis_index("outer").astype(jnp.int32).reshape(1)
    swap = [(i, i ^ 1) for i in range(2 * pairs)]
    outer_groups = [[b ^ OUTER_TURN for b in range(blocks)]]
    inner_groups = [[i ^ INNER_TURN for i in range(2 * pairs)]]
    pair_groups = [[2 * (r ^ PAIR_TURN) + c for r in range(pairs)] for c in range(2)]

    def vmem(*dims, dtype=bf16):
        return pltpu.VMEM(dims, dtype)

    def sems(count):
        return pltpu.SemaphoreType.DMA((count,))

    pair_rows = vmem(2, 2 * tokens, part)
    pair_rows_f32 = vmem(2 * tokens, part, dtype=f32)
    rows = vmem(tokens, width)
    totals_shape = (shape(blocks, slice_rows, HEAD_DIM),)
    half_states = shape(pairs, slice_rows, HEAD_DIM)
    states = shape(2 * pairs, slice_rows, HEAD_DIM)
    pair_tiles = shape(2, 2 * tokens, part)

    out = shape(tokens, width)
    (kv,) = call(
        state_kernel, (states,), (keys, values), LIMITS["state"], unit,
        far=(0, 1), scratch=(rows, rows, sems(2 * groups)),
    )
    kv_parts = exchange(kv, "inner", inner_groups)
    (send,) = call(
        pack_kernel, (shape(4, tokens, part),), (core, query, keys, values, grads), LIMITS["pack"],
        far=(1, 2, 3, 4), smem=(0,), scratch=(sems(4),),
    )
    recv = lax.ppermute(send, "inner", swap)
    (sent,) = call(total_kernel, totals_shape, (kv_parts, send), LIMITS["total"], far=(1,))
    kv_totals = exchange(sent, "outer", outer_groups)
    inner, qg, kv_pair = call(
        local_kernel,
        (shape(2 * tokens, part, dtype=f32), pair_tiles, pair_tiles),
        (core, query, keys, values, grads, recv),
        LIMITS["local"], 4 * unit,
        far=(1, 2, 3, 4, 5), smem=(0,), scratch=(sems(8),),
    )
    (running,) = call(
        prior_kernel, (half_states,), (place, kv_parts, kv_totals, qg), LIMITS["prior"],
        far=(3,), smem=(0,),
    )
    prior = exchange(running, "inner", pair_groups)
    (gq_state,) = call(
        mixed_kernel, (half_states,), (qg, inner, prior), LIMITS["mixed"], 2 * unit,
        far=(1,), scratch=(pair_rows_f32, sems(part_groups)),
    )
    gq_parts = exchange(gq_state, "inner", pair_groups)
    piece = GROUP
    quarter = shape(4, tokens, piece)

    def side(first):
        return call(
            functools.partial(side_kernel, first), (quarter, quarter),
            (core, qg, kv_pair, inner, prior), LIMITS["side"], 5 * unit,
            far=(1, 2, 3, 4), smem=(0,),
            scratch=(
                vmem(2, 2 * tokens, piece), vmem(2, 2 * tokens, piece),
                vmem(2 * tokens, piece, dtype=f32), vmem(pairs, slice_rows, HEAD_DIM),
                vmem(4, 2 * tokens, piece), sems(5), sems(1),
            ),
        )

    own_a, send_a = side(0)
    own_b, send_b = side(piece // HEAD_DIM)
    (sent,) = call(total_kernel, totals_shape, (gq_parts, own_a), LIMITS["total"], far=(1,))
    gq_totals = exchange(sent, "outer", outer_groups)
    recv_a = lax.ppermute(send_a, "inner", swap)
    recv_b = lax.ppermute(send_b, "inner", swap)
    swapped = (own_a, own_b, recv_a, recv_b)
    attended, grad_query = call(
        finish_kernel, (out, out), (core,) + swapped, LIMITS["finish"],
        far=(1, 2, 3, 4), smem=(0,), scratch=(sems(8),),
    )
    (running,) = call(
        later_kernel, (states,), (place, gq_parts, gq_totals, own_b), LIMITS["later"],
        far=(3,), smem=(0,),
    )
    later = exchange(running, "inner", inner_groups)
    grad_key, grad_value = call(
        last_kernel, (out, out), (core, keys, values) + swapped + (later,), LIMITS["last"], 2 * unit,
        far=(3, 4, 5, 6), far_out=(0, 1), smem=(0,),
        scratch=(rows,) * 4 + (sems(8), sems(2 * groups)),
    )
    return attended, grad_query, grad_key, grad_value


def solution(mesh):
    split = Mesh(mesh.devices.reshape(-1, 64), ("outer", "inner"))
    placed = P(("outer", "inner"), None)
    return jax.shard_map(
        per_device,
        mesh=split,
        in_specs=(placed,) * 4,
        out_specs=(placed,) * 4,
        check_vma=False,
    )
```

```python
import functools

import jax
import jax.numpy as jnp
from jax import lax
from jax.experimental import pallas as pl
from jax.experimental.pallas import tpu as pltpu
from jax.sharding import Mesh, PartitionSpec as P

HEAD_DIM = 128
GROUP = 512
MIB = 1024 * 1024
LIMITS = {
    "state": 53 * MIB,
    "pack": 56 * MIB,
    "total": 53 * MIB,
    "local": 51 * MIB,
    "prior": 53 * MIB,
    "mixed": 51 * MIB,
    "side": 56 * MIB,
    "later": 53 * MIB,
    "finish": 48 * MIB,
    "last": 50 * MIB,
}
OUTER_TURN = 4
INNER_TURN = 20
PAIR_TURN = INNER_TURN // 2
f32 = jnp.float32
bf16 = jnp.bfloat16


def dot_nn(a, b):
    return lax.dot_general(a, b, (((1,), (0,)), ((), ())), preferred_element_type=f32)


def dot_nt(a, b):
    return lax.dot_general(a, b, (((1,), (1,)), ((), ())), preferred_element_type=f32)


def dot_tn(a, b):
    return lax.dot_general(a, b, (((0,), (0,)), ((), ())), preferred_element_type=f32)


def shape(*dims, dtype=bf16):
    return jax.ShapeDtypeStruct(dims, dtype)


def call(kernel, out_shape, operands, limit, flops=0, far=(), far_out=(), smem=(), scratch=()):
    def space(i, kept):
        return pl.BlockSpec(memory_space=pltpu.HBM if i in kept else pltpu.VMEM)

    in_specs = [
        pl.BlockSpec(memory_space=pltpu.SMEM) if i in smem else space(i, far)
        for i in range(len(operands))
    ]
    out_specs = tuple(space(i, far_out) for i in range(len(out_shape)))
    moved = sum(x.size * x.dtype.itemsize for x in tuple(operands) + out_shape)
    return pl.pallas_call(
        kernel,
        out_shape=out_shape,
        in_specs=in_specs,
        out_specs=out_specs,
        scratch_shapes=scratch,
        compiler_params=pltpu.CompilerParams(vmem_limit_bytes=limit),
        cost_estimate=pl.CostEstimate(flops=flops, bytes_accessed=moved, transcendentals=0),
    )(*operands)


def copies_of(pairs, sems, first=0):
    return [
        pltpu.make_async_copy(src, dst, sems.at[first + i]) for i, (src, dst) in enumerate(pairs)
    ]


def start_all(copies):
    for copy in copies:
        copy.start()


def wait_all(copies):
    for copy in copies:
        copy.wait()


def columns(g, width=GROUP):
    return pl.ds(g * width, width)


def heads_of(g, width=GROUP):
    heads = range(g * width // HEAD_DIM, (g + 1) * width // HEAD_DIM)
    return [(h, slice(h * HEAD_DIM, (h + 1) * HEAD_DIM)) for h in heads]


def half(ref, which):
    count = ref.shape[-1] // 2
    return ref.at[:, pl.ds(pl.multiple_of(which * count, count), count)]


def rows_of(core, count):
    return pl.ds(pl.multiple_of(core * count, count), count)


def at_or_after(count, turned=False):
    rows = lax.broadcasted_iota(jnp.int32, (count, count), 0)
    cols = lax.broadcasted_iota(jnp.int32, (count, count), 1)
    return cols >= rows if turned else rows >= cols


def state_kernel(k_far, v_far, out_far, k_ref, v_ref, out_ref, sems, out_sems):
    pairs, _, rows, _ = out_far.shape
    cuts = HEAD_DIM // rows
    heads = pairs // cuts
    count = k_far.shape[1] // GROUP
    copies = [
        copies_of(
            [(src.at[:, columns(g)], dst.at[:, columns(g)]) for src, dst in ((k_far, k_ref), (v_far, v_ref))],
            sems, 2 * g,
        )
        for g in range(count)
    ]
    for group in copies:
        start_all(group)
    out_copies = []
    for g, group in enumerate(copies):
        wait_all(group)
        for h, cols in heads_of(g):
            state = dot_tn(k_ref[:, cols], v_ref[:, cols]).astype(bf16)
            for q in range(cuts):
                r = (h % heads) * cuts + q
                out_ref[r ^ PAIR_TURN, h // heads] = state[q * rows : (q + 1) * rows]
        block = pl.ds((g % 2) * (pairs // 2), pairs // 2)
        out_copies += copies_of(
            [(out_ref.at[block, g // 2], out_far.at[block, g // 2])], out_sems, g
        )
        out_copies[-1].start()
    wait_all(out_copies)


def total_kernel(parts_ref, after_far, out_ref):
    total = parts_ref[0].astype(f32)
    for j in range(1, parts_ref.shape[0]):
        total = total + parts_ref[j].astype(f32)
    total = total.astype(bf16)
    for j in range(out_ref.shape[0]):
        out_ref[j] = total


def outer_sum(reverse, place, totals_ref):
    acc = jnp.zeros(totals_ref.shape[1:], f32)
    for b in range(totals_ref.shape[0]):
        wanted = b > place if reverse else b < place
        acc = acc + jnp.where(wanted, totals_ref[b ^ OUTER_TURN].astype(f32), 0.0)
    return acc


def prior_kernel(place_ref, parts_ref, totals_ref, after_far, out_ref):
    acc = outer_sum(False, place_ref[0], totals_ref)
    for r in range(out_ref.shape[0]):
        out_ref[r ^ PAIR_TURN] = acc.astype(bf16)
        for i in (2 * r, 2 * r + 1):
            acc = acc + parts_ref[i ^ INNER_TURN].astype(f32)


def later_kernel(place_ref, parts_ref, totals_ref, out_far, out_ref, out_sems):
    acc = outer_sum(True, place_ref[0], totals_ref)
    pairs = parts_ref.shape[0]
    step = pairs // 4
    out_copies = []
    for r in reversed(range(pairs)):
        for c in range(2):
            out_ref[r ^ PAIR_TURN, c] = acc.astype(bf16)
        acc = acc + parts_ref[r ^ PAIR_TURN].astype(f32)
        if r % step == 0:
            block = pl.ds((r ^ PAIR_TURN) // step * step, step)
            out_copies += copies_of([(out_ref.at[block], out_far.at[block])], out_sems, r // step)
            out_copies[-1].start()
    wait_all(out_copies)


def pack_kernel(core_ref, q_far, k_far, v_far, g_far, out_ref, sems):
    other = 1 - core_ref[0]
    rows = (q_far, k_far, v_far, g_far)
    copies = copies_of([(half(src, other), out_ref.at[i]) for i, src in enumerate(rows)], sems)
    start_all(copies)
    wait_all(copies)


def local_kernel(
    core_ref, q_far, k_far, v_far, g_far, recv_far, inner_far, qg_far, kv_far,
    inner_ref, qg_ref, kv_ref, sems, out_sems,
):
    core = core_ref[0]
    count = q_far.shape[0]
    part = inner_far.shape[1]
    mine, theirs = rows_of(core, count), rows_of(1 - core, count)
    q_ref, k_ref, v_ref = qg_ref.at[0], kv_ref.at[0], kv_ref.at[1]
    near = (q_ref, k_ref, v_ref, qg_ref.at[1])
    copies = []
    for g in range(part // GROUP):
        own = pl.ds(pl.multiple_of(core * part + g * GROUP, GROUP), GROUP)
        pairs = [
            (src.at[:, own], dst.at[mine, columns(g)])
            for src, dst in zip((q_far, k_far, v_far, g_far), near)
        ]
        pairs += [(recv_far.at[i, :, columns(g)], dst.at[theirs, columns(g)]) for i, dst in enumerate(near)]
        copies.append(copies_of(pairs, sems, 8 * g))
    for group in copies:
        start_all(group)
    mask = at_or_after(2 * count)
    out_copies = []
    for g, group in enumerate(copies):
        wait_all(group)
        rows = copies_of(
            [(ref.at[:, :, columns(g)], far.at[:, :, columns(g)]) for ref, far in ((qg_ref, qg_far), (kv_ref, kv_far))],
            out_sems, 3 * g,
        )
        start_all(rows)
        heads = heads_of(g)
        scores = [dot_nt(q_ref[:, cols], k_ref[:, cols]) for _, cols in heads]
        local = [jnp.where(mask, x, 0.0).astype(bf16) for x in scores]
        for (_, cols), x in zip(heads, local):
            inner_ref[:, cols] = dot_nn(x, v_ref[:, cols])
        mixed = copies_of([(inner_ref.at[:, columns(g)], inner_far.at[:, columns(g)])], out_sems, 3 * g + 2)
        start_all(mixed)
        out_copies += rows + mixed
    wait_all(out_copies)


def whole_state(ref, h):
    cuts = HEAD_DIM // ref.shape[1]
    return jnp.concatenate([ref[(h * cuts + q) ^ PAIR_TURN] for q in range(cuts)], axis=0)


def normed_parts(mixed, grad):
    scale = lax.rsqrt(jnp.mean(mixed * mixed, axis=-1, keepdims=True) + 1e-06)
    inner_mean = jnp.mean(grad * mixed, axis=-1, keepdims=True)
    dy = (scale * grad - mixed * (scale * scale * scale * inner_mean)).astype(bf16)
    return scale, dy


def mixed_kernel(qg_ref, inner_far, prior_ref, state_far, inner_ref, state_ref, sems, out_sems):
    pairs, rows, _ = state_ref.shape
    cuts = HEAD_DIM // rows
    q_ref, g_ref = qg_ref.at[0], qg_ref.at[1]
    count = q_ref.shape[1] // GROUP
    copies = copies_of([(inner_far.at[:, columns(g)], inner_ref.at[:, columns(g)]) for g in range(count)], sems)
    start_all(copies)
    out_copies = []
    for g, copy in enumerate(copies):
        copy.wait()
        for h, cols in heads_of(g):
            query = q_ref[:, cols]
            mixed = inner_ref[:, cols] + dot_nn(query, whole_state(prior_ref, h))
            _, dy = normed_parts(mixed, g_ref[:, cols].astype(f32))
            state = dot_tn(query, dy).astype(bf16)
            for q in range(cuts):
                state_ref[(h * cuts + q) ^ PAIR_TURN] = state[q * rows : (q + 1) * rows]
        block = pl.ds(g * (pairs // count), pairs // count)
        out_copies += copies_of([(state_ref.at[block], state_far.at[block])], out_sems, g)
        out_copies[-1].start()
    wait_all(out_copies)


def side_kernel(
    core_ref, qg_far, kv_far, inner_far, prior_far, own_far, send_far,
    qg_ref, kv_ref, inner_ref, prior_ref, tile_ref, sems, prior_sem, out_sems,
):
    core = core_ref[0]
    count = own_far.shape[1]
    q_ref, g_ref, k_ref, v_ref = qg_ref.at[0], qg_ref.at[1], kv_ref.at[0], kv_ref.at[1]
    prior_copy = copies_of([(prior_far, prior_ref)], prior_sem)
    start_all(prior_copy)
    copies = [
        copies_of(
            [
                (qg_far.at[:, :, columns(g)], qg_ref.at[:, :, columns(g)]),
                (inner_far.at[:, columns(g)], inner_ref.at[:, columns(g)]),
                (kv_far.at[:, :, columns(g)], kv_ref.at[:, :, columns(g)]),
            ],
            sems, 3 * g,
        )
        for g in range(inner_ref.shape[1] // GROUP)
    ]
    for group in copies:
        start_all(group)
    mask = at_or_after(2 * count)
    turned = at_or_after(2 * count, True)
    mine, theirs = rows_of(core, count), rows_of(1 - core, count)
    wait_all(prior_copy)
    out_copies = []
    for g, group in enumerate(copies):
        wait_all(group)
        heads = heads_of(g)
        queries = [q_ref[:, cols] for _, cols in heads]
        key_rows = [k_ref[:, cols] for _, cols in heads]
        value_rows = [v_ref[:, cols] for _, cols in heads]
        priors = [whole_state(prior_ref, h) for h, _ in heads]
        mixed = [inner_ref[:, cols] + dot_nn(q, p) for (_, cols), q, p in zip(heads, queries, priors)]
        local_t = [
            jnp.where(turned, dot_nt(k, q), 0.0).astype(bf16) for k, q in zip(key_rows, queries)
        ]
        normed = [normed_parts(x, g_ref[:, cols].astype(f32)) for x, (_, cols) in zip(mixed, heads)]
        dlocal = [
            jnp.where(mask, dot_nt(dy, v), 0.0).astype(bf16) for (_, dy), v in zip(normed, value_rows)
        ]
        dlocal_t = [
            jnp.where(turned, dot_nt(v, dy), 0.0).astype(bf16) for (_, dy), v in zip(normed, value_rows)
        ]
        for i, (_, cols) in enumerate(heads):
            scale, dy = normed[i]
            tile_ref[0, :, cols] = (mixed[i] * scale).astype(bf16)
            tile_ref[1, :, cols] = (dot_nn(dlocal[i], key_rows[i]) + dot_nt(dy, priors[i])).astype(bf16)
            tile_ref[2, :, cols] = dot_nn(dlocal_t[i], queries[i]).astype(bf16)
            tile_ref[3, :, cols] = dot_nn(local_t[i], dy).astype(bf16)
        group_out = copies_of(
            [
                (tile_ref.at[:, mine, columns(g)], own_far.at[:, :, columns(g)]),
                (tile_ref.at[:, theirs, columns(g)], send_far.at[:, :, columns(g)]),
            ],
            out_sems, 2 * g,
        )
        start_all(group_out)
        out_copies += group_out
    wait_all(out_copies)


def swapped_copies(core, first, outs, own_far, recv_far, sems):
    pairs = [(own_far.at[first + i], half(dst, core)) for i, dst in enumerate(outs)]
    pairs += [(recv_far.at[first + i], half(dst, 1 - core)) for i, dst in enumerate(outs)]
    return copies_of(pairs, sems)


def finish_kernel(core_ref, own_far, recv_far, attended_ref, gq_ref, sems):
    copies = swapped_copies(core_ref[0], 0, (attended_ref, gq_ref), own_far, recv_far, sems)
    start_all(copies)
    wait_all(copies)


def last_kernel(
    core_ref, k_ref, v_ref, own_far, recv_far, later_far, out_k_far, out_v_far,
    gk_ref, gv_ref, later_ref, out_k_ref, out_v_ref, sems, later_sem, out_sems,
):
    cuts = HEAD_DIM // later_far.shape[1]
    heads = later_far.shape[0] // cuts // 2
    copies = copies_of([(later_far, later_ref)], later_sem)
    copies += swapped_copies(core_ref[0], 2, (gk_ref, gv_ref), own_far, recv_far, sems)
    start_all(copies)
    wait_all(copies)
    out_copies = []
    for g in range(k_ref.shape[1] // GROUP):
        for h, cols in heads_of(g):
            places = [2 * ((h % heads) * cuts + q) + h // heads for q in range(cuts)]
            later = jnp.concatenate([later_ref[i ^ INNER_TURN] for i in places], axis=0)
            gk = gk_ref[:, cols].astype(f32) + dot_nt(v_ref[:, cols], later)
            gv = gv_ref[:, cols].astype(f32) + dot_nn(k_ref[:, cols], later)
            out_k_ref[:, cols] = gk.astype(bf16)
            out_v_ref[:, cols] = gv.astype(bf16)
        group = copies_of(
            [
                (near.at[:, columns(g)], far.at[:, columns(g)])
                for near, far in ((out_k_ref, out_k_far), (out_v_ref, out_v_far))
            ],
            out_sems, 2 * g,
        )
        start_all(group)
        out_copies += group
    wait_all(out_copies)


def exchange(blocks, axis, groups):
    return lax.all_to_all(blocks, axis, 0, 0, tiled=True, axis_index_groups=groups)


def per_device(query, keys, values, grads):
    tokens, width = query.shape
    part = width // 2
    pairs = lax.axis_size("inner") // 2
    blocks = lax.axis_size("outer")
    slice_rows = part // pairs
    groups = width // GROUP
    part_groups = part // GROUP
    unit = 2 * tokens * width * HEAD_DIM
    core = (lax.axis_index("inner").astype(jnp.int32) % 2).reshape(1)
    place = lax.axis_index("outer").astype(jnp.int32).reshape(1)
    swap = [(i, i ^ 1) for i in range(2 * pairs)]
    outer_groups = [[b ^ OUTER_TURN for b in range(blocks)]]
    inner_groups = [[i ^ INNER_TURN for i in range(2 * pairs)]]
    pair_groups = [[2 * (r ^ PAIR_TURN) + c for r in range(pairs)] for c in range(2)]

    def vmem(*dims, dtype=bf16):
        return pltpu.VMEM(dims, dtype)

    def sems(count):
        return pltpu.SemaphoreType.DMA((count,))

    rows = vmem(tokens, width)
    totals_shape = (shape(blocks, slice_rows, HEAD_DIM),)
    half_states = shape(pairs, slice_rows, HEAD_DIM)
    states = shape(pairs, 2, slice_rows, HEAD_DIM)
    pair_tiles = shape(2, 2 * tokens, part)
    inner_shape = shape(2 * tokens, part, dtype=f32)
    out = shape(tokens, width)

    (kv,) = call(
        state_kernel, (states,), (keys, values), LIMITS["state"], unit,
        far=(0, 1), far_out=(0,),
        scratch=(rows, rows, vmem(*states.shape), sems(2 * groups), sems(groups)),
    )
    kv_parts = exchange(kv.reshape(-1, slice_rows, HEAD_DIM), "inner", inner_groups)
    (send,) = call(
        pack_kernel, (shape(4, tokens, part),), (core, query, keys, values, grads), LIMITS["pack"],
        far=(1, 2, 3, 4), smem=(0,), scratch=(sems(4),),
    )
    recv = lax.ppermute(send, "inner", swap)
    (sent,) = call(total_kernel, totals_shape, (kv_parts, send), LIMITS["total"], far=(1,))
    kv_totals = exchange(sent, "outer", outer_groups)
    inner, qg, kv_pair = call(
        local_kernel, (inner_shape, pair_tiles, pair_tiles),
        (core, query, keys, values, grads, recv), LIMITS["local"], 4 * unit,
        far=(1, 2, 3, 4, 5), far_out=(0, 1, 2), smem=(0,),
        scratch=(
            vmem(2 * tokens, part, dtype=f32), vmem(*pair_tiles.shape), vmem(*pair_tiles.shape),
            sems(8 * part_groups), sems(3 * part_groups),
        ),
    )
    (running,) = call(
        prior_kernel, (half_states,), (place, kv_parts, kv_totals, qg), LIMITS["prior"],
        far=(3,), smem=(0,),
    )
    prior = exchange(running, "inner", pair_groups)
    (gq_state,) = call(
        mixed_kernel, (half_states,), (qg, inner, prior), LIMITS["mixed"], 2 * unit,
        far=(1,), far_out=(0,),
        scratch=(
            vmem(2 * tokens, part, dtype=f32), vmem(*half_states.shape),
            sems(part_groups), sems(part_groups),
        ),
    )
    gq_parts = exchange(gq_state, "inner", pair_groups)
    swapped = shape(4, tokens, part)
    own, send = call(
        side_kernel, (swapped, swapped), (core, qg, kv_pair, inner, prior), LIMITS["side"], 10 * unit,
        far=(1, 2, 3, 4), far_out=(0, 1), smem=(0,),
        scratch=(
            vmem(*pair_tiles.shape), vmem(*pair_tiles.shape), vmem(2 * tokens, part, dtype=f32),
            vmem(*half_states.shape), vmem(4, 2 * tokens, part),
            sems(3 * part_groups), sems(1), sems(2 * part_groups),
        ),
    )
    (sent,) = call(total_kernel, totals_shape, (gq_parts, own), LIMITS["total"], far=(1,))
    gq_totals = exchange(sent, "outer", outer_groups)
    (running,) = call(
        later_kernel, (states,), (place, gq_parts, gq_totals), LIMITS["later"],
        far_out=(0,), smem=(0,), scratch=(vmem(*states.shape), sems(4)),
    )
    later = exchange(running.reshape(-1, slice_rows, HEAD_DIM), "inner", inner_groups)
    recv = lax.ppermute(send, "inner", swap)
    attended, grad_query = call(
        finish_kernel, (out, out), (core, own, recv), LIMITS["finish"],
        far=(1, 2), smem=(0,), scratch=(sems(4),),
    )
    grad_key, grad_value = call(
        last_kernel, (out, out), (core, keys, values, own, recv, later), LIMITS["last"], 2 * unit,
        far=(3, 4, 5), far_out=(0, 1), smem=(0,),
        scratch=(rows, rows, vmem(*later.shape), rows, rows, sems(4), sems(1), sems(2 * groups)),
    )
    return attended, grad_query, grad_key, grad_value


def solution(mesh):
    split = Mesh(mesh.devices.reshape(-1, 64), ("outer", "inner"))
    placed = P(("outer", "inner"), None)
    return jax.shard_map(
        per_device,
        mesh=split,
        in_specs=(placed,) * 4,
        out_specs=(placed,) * 4,
        check_vma=False,
    )
```

```python
import functools

import jax
import jax.numpy as jnp
from jax import lax
from jax.experimental import pallas as pl
from jax.experimental.pallas import tpu as pltpu
from jax.sharding import Mesh, PartitionSpec as P

HEAD_DIM = 128
GROUP = 512
MIB = 1024 * 1024
LIMITS = {
    "state": 53 * MIB,
    "pack": 56 * MIB,
    "total": 53 * MIB,
    "local": 51 * MIB,
    "prior": 53 * MIB,
    "mixed": 50 * MIB,
    "side": 56 * MIB,
    "later": 53 * MIB,
    "finish": 48 * MIB,
    "last": 50 * MIB,
}
OUTER_TURN = 4
INNER_TURN = 53
PAIR_TURN, CORE_TURN = INNER_TURN // 2, INNER_TURN % 2
f32 = jnp.float32
bf16 = jnp.bfloat16


def dot_nn(a, b):
    return lax.dot_general(a, b, (((1,), (0,)), ((), ())), preferred_element_type=f32)


def dot_nt(a, b):
    return lax.dot_general(a, b, (((1,), (1,)), ((), ())), preferred_element_type=f32)


def dot_tn(a, b):
    return lax.dot_general(a, b, (((0,), (0,)), ((), ())), preferred_element_type=f32)


def shape(*dims, dtype=bf16):
    return jax.ShapeDtypeStruct(dims, dtype)


def call(kernel, out_shape, operands, limit, flops=0, far=(), far_out=(), smem=(), scratch=()):
    def space(i, kept):
        return pl.BlockSpec(memory_space=pltpu.HBM if i in kept else pltpu.VMEM)

    in_specs = [
        pl.BlockSpec(memory_space=pltpu.SMEM) if i in smem else space(i, far)
        for i in range(len(operands))
    ]
    out_specs = tuple(space(i, far_out) for i in range(len(out_shape)))
    moved = sum(x.size * x.dtype.itemsize for x in tuple(operands) + out_shape)
    return pl.pallas_call(
        kernel,
        out_shape=out_shape,
        in_specs=in_specs,
        out_specs=out_specs,
        scratch_shapes=scratch,
        compiler_params=pltpu.CompilerParams(vmem_limit_bytes=limit),
        cost_estimate=pl.CostEstimate(flops=flops, bytes_accessed=moved, transcendentals=0),
    )(*operands)


def copies_of(pairs, sems, first=0):
    return [
        pltpu.make_async_copy(src, dst, sems.at[first + i]) for i, (src, dst) in enumerate(pairs)
    ]


def start_all(copies):
    for copy in copies:
        copy.start()


def wait_all(copies):
    for copy in copies:
        copy.wait()


def columns(g, width=GROUP):
    return pl.ds(g * width, width)


def heads_of(g, width=GROUP):
    heads = range(g * width // HEAD_DIM, (g + 1) * width // HEAD_DIM)
    return [(h, slice(h * HEAD_DIM, (h + 1) * HEAD_DIM)) for h in heads]


def half(ref, which):
    count = ref.shape[-1] // 2
    return ref.at[:, pl.ds(pl.multiple_of(which * count, count), count)]


def rows_of(core, count):
    return pl.ds(pl.multiple_of(core * count, count), count)


def turned_block(g, size):
    return pl.ds((g * size) ^ (PAIR_TURN // size * size), size)


def at_or_after(count, turned=False):
    rows = lax.broadcasted_iota(jnp.int32, (count, count), 0)
    cols = lax.broadcasted_iota(jnp.int32, (count, count), 1)
    return cols >= rows if turned else rows >= cols


def state_kernel(k_far, v_far, out_far, k_ref, v_ref, out_ref, sems, out_sems):
    pairs, _, rows, _ = out_far.shape
    cuts = HEAD_DIM // rows
    heads = pairs // cuts
    count = k_far.shape[1] // GROUP
    copies = [
        copies_of(
            [(src.at[:, columns(g)], dst.at[:, columns(g)]) for src, dst in ((k_far, k_ref), (v_far, v_ref))],
            sems, 2 * g,
        )
        for g in range(count)
    ]
    for group in copies:
        start_all(group)
    out_copies = []
    for g, group in enumerate(copies):
        wait_all(group)
        for h, cols in heads_of(g):
            state = dot_tn(k_ref[:, cols], v_ref[:, cols]).astype(bf16)
            for q in range(cuts):
                r = (h % heads) * cuts + q
                out_ref[r ^ PAIR_TURN, h // heads ^ CORE_TURN] = state[q * rows : (q + 1) * rows]
        block, core = turned_block(g % 2, pairs // 2), g // 2 ^ CORE_TURN
        out_copies += copies_of(
            [(out_ref.at[block, core], out_far.at[block, core])], out_sems, g
        )
        out_copies[-1].start()
    wait_all(out_copies)


def total_kernel(parts_ref, after_far, out_ref):
    total = parts_ref[0].astype(f32)
    for j in range(1, parts_ref.shape[0]):
        total = total + parts_ref[j].astype(f32)
    total = total.astype(bf16)
    for j in range(out_ref.shape[0]):
        out_ref[j] = total


def outer_sum(reverse, place, totals_ref):
    acc = jnp.zeros(totals_ref.shape[1:], f32)
    for b in range(totals_ref.shape[0]):
        wanted = b > place if reverse else b < place
        acc = acc + jnp.where(wanted, totals_ref[b ^ OUTER_TURN].astype(f32), 0.0)
    return acc


def prior_kernel(place_ref, parts_ref, totals_ref, after_far, out_ref):
    acc = outer_sum(False, place_ref[0], totals_ref)
    for r in range(out_ref.shape[0]):
        out_ref[r ^ PAIR_TURN] = acc.astype(bf16)
        for i in (2 * r, 2 * r + 1):
            acc = acc + parts_ref[i ^ INNER_TURN].astype(f32)


def later_kernel(place_ref, parts_ref, totals_ref, out_far, out_ref, out_sems):
    acc = outer_sum(True, place_ref[0], totals_ref)
    pairs = parts_ref.shape[0]
    step = pairs // 4
    out_copies = []
    for r in reversed(range(pairs)):
        for c in range(2):
            out_ref[r ^ PAIR_TURN, c] = acc.astype(bf16)
        acc = acc + parts_ref[r ^ PAIR_TURN].astype(f32)
        if r % step == 0:
            block = pl.ds((r ^ PAIR_TURN) // step * step, step)
            out_copies += copies_of([(out_ref.at[block], out_far.at[block])], out_sems, r // step)
            out_copies[-1].start()
    wait_all(out_copies)


def pack_kernel(core_ref, q_far, k_far, v_far, g_far, out_ref, sems):
    other = 1 - core_ref[0]
    rows = (q_far, k_far, v_far, g_far)
    copies = copies_of([(half(src, other), out_ref.at[i]) for i, src in enumerate(rows)], sems)
    start_all(copies)
    wait_all(copies)


def local_kernel(
    core_ref, q_far, k_far, v_far, g_far, recv_far, inner_far, qg_far, kv_far,
    inner_ref, qg_ref, kv_ref, sems, out_sems,
):
    core = core_ref[0]
    count = q_far.shape[0]
    part = inner_far.shape[1]
    mine, theirs = rows_of(core, count), rows_of(1 - core, count)
    q_ref, k_ref, v_ref = qg_ref.at[0], kv_ref.at[0], kv_ref.at[1]
    near = (q_ref, k_ref, v_ref, qg_ref.at[1])
    copies = []
    for g in range(part // GROUP):
        own = pl.ds(pl.multiple_of(core * part + g * GROUP, GROUP), GROUP)
        pairs = [
            (src.at[:, own], dst.at[mine, columns(g)])
            for src, dst in zip((q_far, k_far, v_far, g_far), near)
        ]
        pairs += [(recv_far.at[i, :, columns(g)], dst.at[theirs, columns(g)]) for i, dst in enumerate(near)]
        copies.append(copies_of(pairs, sems, 8 * g))
    for group in copies:
        start_all(group)
    mask = at_or_after(2 * count)
    out_copies = []
    for g, group in enumerate(copies):
        wait_all(group)
        rows = copies_of(
            [(ref.at[:, :, columns(g)], far.at[:, :, columns(g)]) for ref, far in ((qg_ref, qg_far), (kv_ref, kv_far))],
            out_sems, 3 * g,
        )
        start_all(rows)
        heads = heads_of(g)
        scores = [dot_nt(q_ref[:, cols], k_ref[:, cols]) for _, cols in heads]
        local = [jnp.where(mask, x, 0.0).astype(bf16) for x in scores]
        for (_, cols), x in zip(heads, local):
            inner_ref[:, cols] = dot_nn(x, v_ref[:, cols])
        mixed = copies_of([(inner_ref.at[:, columns(g)], inner_far.at[:, columns(g)])], out_sems, 3 * g + 2)
        start_all(mixed)
        out_copies += rows + mixed
    wait_all(out_copies)


def whole_state(ref, h):
    cuts = HEAD_DIM // ref.shape[1]
    return jnp.concatenate([ref[(h * cuts + q) ^ PAIR_TURN] for q in range(cuts)], axis=0)


def normed_parts(mixed, grad):
    scale = lax.rsqrt(jnp.mean(mixed * mixed, axis=-1, keepdims=True) + 1e-06)
    inner_mean = jnp.mean(grad * mixed, axis=-1, keepdims=True)
    dy = (scale * grad - mixed * (scale * scale * scale * inner_mean)).astype(bf16)
    return scale, dy


def mixed_kernel(qg_ref, inner_ref, prior_ref, state_far, state_ref, out_sems):
    pairs, rows, _ = state_ref.shape
    cuts = HEAD_DIM // rows
    q_ref, g_ref = qg_ref.at[0], qg_ref.at[1]
    count = q_ref.shape[1] // GROUP
    out_copies = []
    for g in range(count):
        for h, cols in heads_of(g):
            query = q_ref[:, cols]
            mixed = inner_ref[:, cols] + dot_nn(query, whole_state(prior_ref, h))
            _, dy = normed_parts(mixed, g_ref[:, cols].astype(f32))
            state = dot_tn(query, dy).astype(bf16)
            for q in range(cuts):
                state_ref[(h * cuts + q) ^ PAIR_TURN] = state[q * rows : (q + 1) * rows]
        block = turned_block(g, pairs // count)
        out_copies += copies_of([(state_ref.at[block], state_far.at[block])], out_sems, g)
        out_copies[-1].start()
    wait_all(out_copies)


def side_kernel(
    core_ref, qg_far, kv_far, inner_far, prior_far, own_far, send_far,
    qg_ref, kv_ref, inner_ref, prior_ref, tile_ref, sems, prior_sem, out_sems,
):
    core = core_ref[0]
    count = own_far.shape[1]
    q_ref, g_ref, k_ref, v_ref = qg_ref.at[0], qg_ref.at[1], kv_ref.at[0], kv_ref.at[1]
    prior_copy = copies_of([(prior_far, prior_ref)], prior_sem)
    start_all(prior_copy)
    copies = [
        copies_of(
            [
                (qg_far.at[:, :, columns(g)], qg_ref.at[:, :, columns(g)]),
                (inner_far.at[:, columns(g)], inner_ref.at[:, columns(g)]),
                (kv_far.at[:, :, columns(g)], kv_ref.at[:, :, columns(g)]),
            ],
            sems, 3 * g,
        )
        for g in range(inner_ref.shape[1] // GROUP)
    ]
    for group in copies:
        start_all(group)
    mask = at_or_after(2 * count)
    turned = at_or_after(2 * count, True)
    mine, theirs = rows_of(core, count), rows_of(1 - core, count)
    wait_all(prior_copy)
    out_copies = []
    for g, group in enumerate(copies):
        wait_all(group)
        heads = heads_of(g)
        queries = [q_ref[:, cols] for _, cols in heads]
        key_rows = [k_ref[:, cols] for _, cols in heads]
        value_rows = [v_ref[:, cols] for _, cols in heads]
        priors = [whole_state(prior_ref, h) for h, _ in heads]
        mixed = [inner_ref[:, cols] + dot_nn(q, p) for (_, cols), q, p in zip(heads, queries, priors)]
        local_t = [
            jnp.where(turned, dot_nt(k, q), 0.0).astype(bf16) for k, q in zip(key_rows, queries)
        ]
        normed = [normed_parts(x, g_ref[:, cols].astype(f32)) for x, (_, cols) in zip(mixed, heads)]
        dlocal = [
            jnp.where(mask, dot_nt(dy, v), 0.0).astype(bf16) for (_, dy), v in zip(normed, value_rows)
        ]
        dlocal_t = [
            jnp.where(turned, dot_nt(v, dy), 0.0).astype(bf16) for (_, dy), v in zip(normed, value_rows)
        ]
        results = (
            lambda i: mixed[i] * normed[i][0],
            lambda i: dot_nn(dlocal[i], key_rows[i]) + dot_nt(normed[i][1], priors[i]),
            lambda i: dot_nn(dlocal_t[i], queries[i]),
            lambda i: dot_nn(local_t[i], normed[i][1]),
        )
        for slot, result in enumerate(results):
            for i, (_, cols) in enumerate(heads):
                tile_ref[slot, :, cols] = result(i).astype(bf16)
            slot_out = copies_of(
                [
                    (tile_ref.at[slot, mine, columns(g)], own_far.at[slot, :, columns(g)]),
                    (tile_ref.at[slot, theirs, columns(g)], send_far.at[slot, :, columns(g)]),
                ],
                out_sems, 2 * (len(results) * g + slot),
            )
            start_all(slot_out)
            out_copies += slot_out
    wait_all(out_copies)


def swapped_copies(core, first, outs, own_far, recv_far, sems):
    pairs = [(own_far.at[first + i], half(dst, core)) for i, dst in enumerate(outs)]
    pairs += [(recv_far.at[first + i], half(dst, 1 - core)) for i, dst in enumerate(outs)]
    return copies_of(pairs, sems)


def finish_kernel(core_ref, own_far, recv_far, attended_ref, gq_ref, sems):
    copies = swapped_copies(core_ref[0], 0, (attended_ref, gq_ref), own_far, recv_far, sems)
    start_all(copies)
    wait_all(copies)


def last_kernel(
    core_ref, k_ref, v_ref, own_far, recv_far, later_far, out_k_far, out_v_far,
    gk_ref, gv_ref, later_ref, out_k_ref, out_v_ref, sems, later_sem, out_sems,
):
    cuts = HEAD_DIM // later_far.shape[1]
    heads = later_far.shape[0] // cuts // 2
    copies = copies_of([(later_far, later_ref)], later_sem)
    copies += swapped_copies(core_ref[0], 2, (gk_ref, gv_ref), own_far, recv_far, sems)
    start_all(copies)
    wait_all(copies)
    out_copies = []
    for g in range(k_ref.shape[1] // GROUP):
        for h, cols in heads_of(g):
            places = [2 * ((h % heads) * cuts + q) + h // heads for q in range(cuts)]
            later = jnp.concatenate([later_ref[i ^ INNER_TURN] for i in places], axis=0)
            gk = gk_ref[:, cols].astype(f32) + dot_nt(v_ref[:, cols], later)
            gv = gv_ref[:, cols].astype(f32) + dot_nn(k_ref[:, cols], later)
            out_k_ref[:, cols] = gk.astype(bf16)
            out_v_ref[:, cols] = gv.astype(bf16)
        group = copies_of(
            [
                (near.at[:, columns(g)], far.at[:, columns(g)])
                for near, far in ((out_k_ref, out_k_far), (out_v_ref, out_v_far))
            ],
            out_sems, 2 * g,
        )
        start_all(group)
        out_copies += group
    wait_all(out_copies)


def exchange(blocks, axis, groups):
    return lax.all_to_all(blocks, axis, 0, 0, tiled=True, axis_index_groups=groups)


def per_device(query, keys, values, grads):
    tokens, width = query.shape
    part = width // 2
    pairs = lax.axis_size("inner") // 2
    blocks = lax.axis_size("outer")
    slice_rows = part // pairs
    groups = width // GROUP
    part_groups = part // GROUP
    unit = 2 * tokens * width * HEAD_DIM
    core = (lax.axis_index("inner").astype(jnp.int32) % 2).reshape(1)
    place = lax.axis_index("outer").astype(jnp.int32).reshape(1)
    swap = [(i, i ^ 1) for i in range(2 * pairs)]
    outer_groups = [[b ^ OUTER_TURN for b in range(blocks)]]
    inner_groups = [[i ^ INNER_TURN for i in range(2 * pairs)]]
    pair_groups = [[2 * (r ^ PAIR_TURN) + c for r in range(pairs)] for c in range(2)]

    def vmem(*dims, dtype=bf16):
        return pltpu.VMEM(dims, dtype)

    def sems(count):
        return pltpu.SemaphoreType.DMA((count,))

    rows = vmem(tokens, width)
    totals_shape = (shape(blocks, slice_rows, HEAD_DIM),)
    half_states = shape(pairs, slice_rows, HEAD_DIM)
    states = shape(pairs, 2, slice_rows, HEAD_DIM)
    pair_tiles = shape(2, 2 * tokens, part)
    inner_shape = shape(2 * tokens, part, dtype=f32)
    out = shape(tokens, width)

    (kv,) = call(
        state_kernel, (states,), (keys, values), LIMITS["state"], unit,
        far=(0, 1), far_out=(0,),
        scratch=(rows, rows, vmem(*states.shape), sems(2 * groups), sems(groups)),
    )
    kv_parts = exchange(kv.reshape(-1, slice_rows, HEAD_DIM), "inner", inner_groups)
    (send,) = call(
        pack_kernel, (shape(4, tokens, part),), (core, query, keys, values, grads), LIMITS["pack"],
        far=(1, 2, 3, 4), smem=(0,), scratch=(sems(4),),
    )
    recv = lax.ppermute(send, "inner", swap)
    (sent,) = call(total_kernel, totals_shape, (kv_parts, send), LIMITS["total"], far=(1,))
    kv_totals = exchange(sent, "outer", outer_groups)
    inner, qg, kv_pair = call(
        local_kernel, (inner_shape, pair_tiles, pair_tiles),
        (core, query, keys, values, grads, recv), LIMITS["local"], 4 * unit,
        far=(1, 2, 3, 4, 5), far_out=(0, 1, 2), smem=(0,),
        scratch=(
            vmem(2 * tokens, part, dtype=f32), vmem(*pair_tiles.shape), vmem(*pair_tiles.shape),
            sems(8 * part_groups), sems(3 * part_groups),
        ),
    )
    (running,) = call(
        prior_kernel, (half_states,), (place, kv_parts, kv_totals, qg), LIMITS["prior"],
        far=(3,), smem=(0,),
    )
    prior = exchange(running, "inner", pair_groups)
    (gq_state,) = call(
        mixed_kernel, (half_states,), (qg, inner, prior), LIMITS["mixed"], 2 * unit,
        far_out=(0,), scratch=(vmem(*half_states.shape), sems(part_groups)),
    )
    gq_parts = exchange(gq_state, "inner", pair_groups)
    swapped = shape(4, tokens, part)
    own, send = call(
        side_kernel, (swapped, swapped), (core, qg, kv_pair, inner, prior), LIMITS["side"], 10 * unit,
        far=(1, 2, 3, 4), far_out=(0, 1), smem=(0,),
        scratch=(
            vmem(*pair_tiles.shape), vmem(*pair_tiles.shape), vmem(2 * tokens, part, dtype=f32),
            vmem(*half_states.shape), vmem(4, 2 * tokens, part),
            sems(3 * part_groups), sems(1), sems(8 * part_groups),
        ),
    )
    (sent,) = call(total_kernel, totals_shape, (gq_parts, own), LIMITS["total"], far=(1,))
    gq_totals = exchange(sent, "outer", outer_groups)
    (running,) = call(
        later_kernel, (states,), (place, gq_parts, gq_totals), LIMITS["later"],
        far_out=(0,), smem=(0,), scratch=(vmem(*states.shape), sems(4)),
    )
    later = exchange(running.reshape(-1, slice_rows, HEAD_DIM), "inner", inner_groups)
    recv = lax.ppermute(send, "inner", swap)
    attended, grad_query = call(
        finish_kernel, (out, out), (core, own, recv), LIMITS["finish"],
        far=(1, 2), smem=(0,), scratch=(sems(4),),
    )
    grad_key, grad_value = call(
        last_kernel, (out, out), (core, keys, values, own, recv, later), LIMITS["last"], 2 * unit,
        far=(3, 4, 5), far_out=(0, 1), smem=(0,),
        scratch=(rows, rows, vmem(*later.shape), rows, rows, sems(4), sems(1), sems(2 * groups)),
    )
    return attended, grad_query, grad_key, grad_value


def solution(mesh):
    split = Mesh(mesh.devices.reshape(-1, 64), ("outer", "inner"))
    placed = P(("outer", "inner"), None)
    return jax.shard_map(
        per_device,
        mesh=split,
        in_specs=(placed,) * 4,
        out_specs=(placed,) * 4,
        check_vma=False,
    )
```

```python
import functools

import jax
import jax.numpy as jnp
from jax import lax
from jax.experimental import pallas as pl
from jax.experimental.pallas import tpu as pltpu
from jax.sharding import Mesh, PartitionSpec as P

HEAD_DIM = 128
GROUP = 512
MIB = 1024 * 1024
LIMITS = {
    "state": 53 * MIB,
    "pack": 56 * MIB,
    "total": 53 * MIB,
    "local": 51 * MIB,
    "prior": 53 * MIB,
    "mixed": 50 * MIB,
    "side": 56 * MIB,
    "later": 53 * MIB,
    "finish": 48 * MIB,
    "last": 50 * MIB,
}
OUTER_TURN = 4
INNER_TURN = 53
PAIR_TURN, CORE_TURN = INNER_TURN // 2, INNER_TURN % 2
f32 = jnp.float32
bf16 = jnp.bfloat16


def dot_nn(a, b):
    return lax.dot_general(a, b, (((1,), (0,)), ((), ())), preferred_element_type=f32)


def dot_nt(a, b):
    return lax.dot_general(a, b, (((1,), (1,)), ((), ())), preferred_element_type=f32)


def dot_tn(a, b):
    return lax.dot_general(a, b, (((0,), (0,)), ((), ())), preferred_element_type=f32)


def shape(*dims, dtype=bf16):
    return jax.ShapeDtypeStruct(dims, dtype)


def call(kernel, out_shape, operands, limit, flops=0, far=(), far_out=(), smem=(), scratch=()):
    def space(i, kept):
        return pl.BlockSpec(memory_space=pltpu.HBM if i in kept else pltpu.VMEM)

    in_specs = [
        pl.BlockSpec(memory_space=pltpu.SMEM) if i in smem else space(i, far)
        for i in range(len(operands))
    ]
    out_specs = tuple(space(i, far_out) for i in range(len(out_shape)))
    moved = sum(x.size * x.dtype.itemsize for x in tuple(operands) + out_shape)
    return pl.pallas_call(
        kernel,
        out_shape=out_shape,
        in_specs=in_specs,
        out_specs=out_specs,
        scratch_shapes=scratch,
        compiler_params=pltpu.CompilerParams(vmem_limit_bytes=limit),
        cost_estimate=pl.CostEstimate(flops=flops, bytes_accessed=moved, transcendentals=0),
    )(*operands)


def copies_of(pairs, sems, first=0):
    return [
        pltpu.make_async_copy(src, dst, sems.at[first + i]) for i, (src, dst) in enumerate(pairs)
    ]


def start_all(copies):
    for copy in copies:
        copy.start()


def wait_all(copies):
    for copy in copies:
        copy.wait()


def columns(g, width=GROUP):
    return pl.ds(g * width, width)


def heads_of(g, width=GROUP):
    heads = range(g * width // HEAD_DIM, (g + 1) * width // HEAD_DIM)
    return [(h, slice(h * HEAD_DIM, (h + 1) * HEAD_DIM)) for h in heads]


def half(ref, which):
    count = ref.shape[-1] // 2
    return ref.at[:, pl.ds(pl.multiple_of(which * count, count), count)]


def rows_of(core, count):
    return pl.ds(pl.multiple_of(core * count, count), count)


def turned_block(g, size):
    return pl.ds((g * size) ^ (PAIR_TURN // size * size), size)


def at_or_after(count, turned=False):
    rows = lax.broadcasted_iota(jnp.int32, (count, count), 0)
    cols = lax.broadcasted_iota(jnp.int32, (count, count), 1)
    return cols >= rows if turned else rows >= cols


def state_kernel(k_far, v_far, out_far, k_ref, v_ref, out_ref, sems, out_sems):
    pairs, _, rows, _ = out_far.shape
    cuts = HEAD_DIM // rows
    heads = pairs // cuts
    count = k_far.shape[1] // GROUP
    copies = [
        copies_of(
            [(src.at[:, columns(g)], dst.at[:, columns(g)]) for src, dst in ((k_far, k_ref), (v_far, v_ref))],
            sems, 2 * g,
        )
        for g in range(count)
    ]
    for group in copies:
        start_all(group)
    out_copies = []
    for g, group in enumerate(copies):
        wait_all(group)
        for h, cols in heads_of(g):
            state = dot_tn(k_ref[:, cols], v_ref[:, cols]).astype(bf16)
            for q in range(cuts):
                r = (h % heads) * cuts + q
                out_ref[r ^ PAIR_TURN, h // heads ^ CORE_TURN] = state[q * rows : (q + 1) * rows]
        block, core = turned_block(g % 2, pairs // 2), g // 2 ^ CORE_TURN
        out_copies += copies_of(
            [(out_ref.at[block, core], out_far.at[block, core])], out_sems, g
        )
        out_copies[-1].start()
    wait_all(out_copies)


def total_kernel(parts_ref, after_far, out_ref):
    total = parts_ref[0].astype(f32)
    for j in range(1, parts_ref.shape[0]):
        total = total + parts_ref[j].astype(f32)
    total = total.astype(bf16)
    for j in range(out_ref.shape[0]):
        out_ref[j] = total


def outer_sum(reverse, place, totals_ref):
    acc = jnp.zeros(totals_ref.shape[1:], f32)
    for b in range(totals_ref.shape[0]):
        wanted = b > place if reverse else b < place
        acc = acc + jnp.where(wanted, totals_ref[b ^ OUTER_TURN].astype(f32), 0.0)
    return acc


def prior_kernel(place_ref, parts_ref, totals_ref, after_far, out_ref):
    acc = outer_sum(False, place_ref[0], totals_ref)
    for r in range(out_ref.shape[0]):
        out_ref[r ^ PAIR_TURN] = acc.astype(bf16)
        for i in (2 * r, 2 * r + 1):
            acc = acc + parts_ref[i ^ INNER_TURN].astype(f32)


def later_kernel(place_ref, parts_ref, totals_ref, out_far, out_ref, out_sems):
    acc = outer_sum(True, place_ref[0], totals_ref)
    pairs = parts_ref.shape[0]
    step = pairs // 4
    out_copies = []
    for r in reversed(range(pairs)):
        for c in range(2):
            out_ref[r ^ PAIR_TURN, c] = acc.astype(bf16)
        acc = acc + parts_ref[r ^ PAIR_TURN].astype(f32)
        if r % step == 0:
            block = pl.ds((r ^ PAIR_TURN) // step * step, step)
            out_copies += copies_of([(out_ref.at[block], out_far.at[block])], out_sems, r // step)
            out_copies[-1].start()
    wait_all(out_copies)


def pack_kernel(core_ref, q_far, k_far, v_far, g_far, out_far, near_ref, sems, out_sems):
    other = 1 - core_ref[0]
    rows = (q_far, k_far, v_far, g_far)
    copies = copies_of([(half(src, other), near_ref.at[i]) for i, src in enumerate(rows)], sems)
    start_all(copies)
    out_copies = copies_of([(near_ref.at[i], out_far.at[i]) for i in range(len(rows))], out_sems)
    for copy, out_copy in zip(copies, out_copies):
        copy.wait()
        out_copy.start()
    wait_all(out_copies)


def local_kernel(
    core_ref, q_far, k_far, v_far, g_far, recv_far, inner_far, qg_far, kv_far,
    inner_ref, qg_ref, kv_ref, sems, out_sems,
):
    core = core_ref[0]
    count = q_far.shape[0]
    part = inner_far.shape[1]
    mine, theirs = rows_of(core, count), rows_of(1 - core, count)
    q_ref, k_ref, v_ref = qg_ref.at[0], kv_ref.at[0], kv_ref.at[1]
    near = (q_ref, k_ref, v_ref, qg_ref.at[1])
    copies = []
    for g in range(part // GROUP):
        own = pl.ds(pl.multiple_of(core * part + g * GROUP, GROUP), GROUP)
        pairs = [
            (src.at[:, own], dst.at[mine, columns(g)])
            for src, dst in zip((q_far, k_far, v_far, g_far), near)
        ]
        pairs += [(recv_far.at[i, :, columns(g)], dst.at[theirs, columns(g)]) for i, dst in enumerate(near)]
        copies.append(copies_of(pairs, sems, 8 * g))
    for group in copies:
        start_all(group)
    mask = at_or_after(2 * count)
    out_copies = []
    for g, group in enumerate(copies):
        wait_all(group)
        rows = copies_of(
            [(ref.at[:, :, columns(g)], far.at[:, :, columns(g)]) for ref, far in ((qg_ref, qg_far), (kv_ref, kv_far))],
            out_sems, 3 * g,
        )
        start_all(rows)
        heads = heads_of(g)
        scores = [dot_nt(q_ref[:, cols], k_ref[:, cols]) for _, cols in heads]
        local = [jnp.where(mask, x, 0.0).astype(bf16) for x in scores]
        for (_, cols), x in zip(heads, local):
            inner_ref[:, cols] = dot_nn(x, v_ref[:, cols])
        mixed = copies_of([(inner_ref.at[:, columns(g)], inner_far.at[:, columns(g)])], out_sems, 3 * g + 2)
        start_all(mixed)
        out_copies += rows + mixed
    wait_all(out_copies)


def whole_state(ref, h):
    cuts = HEAD_DIM // ref.shape[1]
    return jnp.concatenate([ref[(h * cuts + q) ^ PAIR_TURN] for q in range(cuts)], axis=0)


def normed_parts(mixed, grad):
    scale = lax.rsqrt(jnp.mean(mixed * mixed, axis=-1, keepdims=True) + 1e-06)
    inner_mean = jnp.mean(grad * mixed, axis=-1, keepdims=True)
    dy = (scale * grad - mixed * (scale * scale * scale * inner_mean)).astype(bf16)
    return scale, dy


def mixed_kernel(qg_ref, inner_ref, prior_ref, state_far, state_ref, out_sems):
    pairs, rows, _ = state_ref.shape
    cuts = HEAD_DIM // rows
    q_ref, g_ref = qg_ref.at[0], qg_ref.at[1]
    count = q_ref.shape[1] // GROUP
    out_copies = []
    for g in range(count):
        for h, cols in heads_of(g):
            query = q_ref[:, cols]
            mixed = inner_ref[:, cols] + dot_nn(query, whole_state(prior_ref, h))
            _, dy = normed_parts(mixed, g_ref[:, cols].astype(f32))
            state = dot_tn(query, dy).astype(bf16)
            for q in range(cuts):
                state_ref[(h * cuts + q) ^ PAIR_TURN] = state[q * rows : (q + 1) * rows]
        block = turned_block(g, pairs // count)
        out_copies += copies_of([(state_ref.at[block], state_far.at[block])], out_sems, g)
        out_copies[-1].start()
    wait_all(out_copies)


def side_kernel(
    core_ref, qg_far, kv_far, inner_far, prior_far, own_far, send_far,
    qg_ref, kv_ref, inner_ref, prior_ref, tile_ref, sems, prior_sem, out_sems,
):
    core = core_ref[0]
    count = own_far.shape[1]
    q_ref, g_ref, k_ref, v_ref = qg_ref.at[0], qg_ref.at[1], kv_ref.at[0], kv_ref.at[1]
    prior_copy = copies_of([(prior_far, prior_ref)], prior_sem)
    start_all(prior_copy)
    copies = [
        copies_of(
            [
                (qg_far.at[:, :, columns(g)], qg_ref.at[:, :, columns(g)]),
                (inner_far.at[:, columns(g)], inner_ref.at[:, columns(g)]),
                (kv_far.at[:, :, columns(g)], kv_ref.at[:, :, columns(g)]),
            ],
            sems, 3 * g,
        )
        for g in range(inner_ref.shape[1] // GROUP)
    ]
    for group in copies:
        start_all(group)
    mask = at_or_after(2 * count)
    turned = at_or_after(2 * count, True)
    mine, theirs = rows_of(core, count), rows_of(1 - core, count)
    wait_all(prior_copy)
    out_copies = []
    for g, group in enumerate(copies):
        wait_all(group)
        heads = heads_of(g)
        queries = [q_ref[:, cols] for _, cols in heads]
        key_rows = [k_ref[:, cols] for _, cols in heads]
        value_rows = [v_ref[:, cols] for _, cols in heads]
        priors = [whole_state(prior_ref, h) for h, _ in heads]
        mixed = [inner_ref[:, cols] + dot_nn(q, p) for (_, cols), q, p in zip(heads, queries, priors)]
        local_t = [
            jnp.where(turned, dot_nt(k, q), 0.0).astype(bf16) for k, q in zip(key_rows, queries)
        ]
        normed = [normed_parts(x, g_ref[:, cols].astype(f32)) for x, (_, cols) in zip(mixed, heads)]
        dlocal = [
            jnp.where(mask, dot_nt(dy, v), 0.0).astype(bf16) for (_, dy), v in zip(normed, value_rows)
        ]
        dlocal_t = [
            jnp.where(turned, dot_nt(v, dy), 0.0).astype(bf16) for (_, dy), v in zip(normed, value_rows)
        ]
        results = (
            lambda i: mixed[i] * normed[i][0],
            lambda i: dot_nn(dlocal[i], key_rows[i]) + dot_nt(normed[i][1], priors[i]),
            lambda i: dot_nn(dlocal_t[i], queries[i]),
            lambda i: dot_nn(local_t[i], normed[i][1]),
        )
        for slot, result in enumerate(results):
            for i, (_, cols) in enumerate(heads):
                tile_ref[slot, :, cols] = result(i).astype(bf16)
            slot_out = copies_of(
                [
                    (tile_ref.at[slot, mine, columns(g)], own_far.at[slot, :, columns(g)]),
                    (tile_ref.at[slot, theirs, columns(g)], send_far.at[slot, :, columns(g)]),
                ],
                out_sems, 2 * (len(results) * g + slot),
            )
            start_all(slot_out)
            out_copies += slot_out
    wait_all(out_copies)


def swapped_copies(core, first, outs, own_far, recv_far, sems):
    pairs = [(own_far.at[first + i], half(dst, core)) for i, dst in enumerate(outs)]
    pairs += [(recv_far.at[first + i], half(dst, 1 - core)) for i, dst in enumerate(outs)]
    return copies_of(pairs, sems)


def finish_kernel(core_ref, own_far, recv_far, attended_ref, gq_ref, sems):
    copies = swapped_copies(core_ref[0], 0, (attended_ref, gq_ref), own_far, recv_far, sems)
    start_all(copies)
    wait_all(copies)


def last_kernel(
    core_ref, k_ref, v_ref, own_far, recv_far, later_far, out_k_far, out_v_far,
    gk_ref, gv_ref, later_ref, out_k_ref, out_v_ref, sems, later_sem, out_sems,
):
    cuts = HEAD_DIM // later_far.shape[1]
    heads = later_far.shape[0] // cuts // 2
    copies = copies_of([(later_far, later_ref)], later_sem)
    copies += swapped_copies(core_ref[0], 2, (gk_ref, gv_ref), own_far, recv_far, sems)
    start_all(copies)
    wait_all(copies)
    out_copies = []
    for g in range(k_ref.shape[1] // GROUP):
        for h, cols in heads_of(g):
            places = [2 * ((h % heads) * cuts + q) + h // heads for q in range(cuts)]
            later = jnp.concatenate([later_ref[i ^ INNER_TURN] for i in places], axis=0)
            gk = gk_ref[:, cols].astype(f32) + dot_nt(v_ref[:, cols], later)
            gv = gv_ref[:, cols].astype(f32) + dot_nn(k_ref[:, cols], later)
            out_k_ref[:, cols] = gk.astype(bf16)
            out_v_ref[:, cols] = gv.astype(bf16)
        group = copies_of(
            [
                (near.at[:, columns(g)], far.at[:, columns(g)])
                for near, far in ((out_k_ref, out_k_far), (out_v_ref, out_v_far))
            ],
            out_sems, 2 * g,
        )
        start_all(group)
        out_copies += group
    wait_all(out_copies)


def exchange(blocks, axis, groups):
    return lax.all_to_all(blocks, axis, 0, 0, tiled=True, axis_index_groups=groups)


def per_device(query, keys, values, grads):
    tokens, width = query.shape
    part = width // 2
    pairs = lax.axis_size("inner") // 2
    blocks = lax.axis_size("outer")
    slice_rows = part // pairs
    groups = width // GROUP
    part_groups = part // GROUP
    unit = 2 * tokens * width * HEAD_DIM
    core = (lax.axis_index("inner").astype(jnp.int32) % 2).reshape(1)
    place = lax.axis_index("outer").astype(jnp.int32).reshape(1)
    swap = [(i, i ^ 1) for i in range(2 * pairs)]
    outer_groups = [[b ^ OUTER_TURN for b in range(blocks)]]
    inner_groups = [[i ^ INNER_TURN for i in range(2 * pairs)]]
    pair_groups = [[2 * (r ^ PAIR_TURN) + c for r in range(pairs)] for c in range(2)]

    def vmem(*dims, dtype=bf16):
        return pltpu.VMEM(dims, dtype)

    def sems(count):
        return pltpu.SemaphoreType.DMA((count,))

    rows = vmem(tokens, width)
    totals_shape = (shape(blocks, slice_rows, HEAD_DIM),)
    half_states = shape(pairs, slice_rows, HEAD_DIM)
    states = shape(pairs, 2, slice_rows, HEAD_DIM)
    pair_tiles = shape(2, 2 * tokens, part)
    inner_shape = shape(2 * tokens, part, dtype=f32)
    out = shape(tokens, width)

    (kv,) = call(
        state_kernel, (states,), (keys, values), LIMITS["state"], unit,
        far=(0, 1), far_out=(0,),
        scratch=(rows, rows, vmem(*states.shape), sems(2 * groups), sems(groups)),
    )
    kv_parts = exchange(kv.reshape(-1, slice_rows, HEAD_DIM), "inner", inner_groups)
    (send,) = call(
        pack_kernel, (shape(4, tokens, part),), (core, query, keys, values, grads), LIMITS["pack"],
        far=(1, 2, 3, 4), far_out=(0,), smem=(0,),
        scratch=(vmem(4, tokens, part), sems(4), sems(4)),
    )
    recv = lax.ppermute(send, "inner", swap)
    (sent,) = call(total_kernel, totals_shape, (kv_parts, send), LIMITS["total"], far=(1,))
    kv_totals = exchange(sent, "outer", outer_groups)
    inner, qg, kv_pair = call(
        local_kernel, (inner_shape, pair_tiles, pair_tiles),
        (core, query, keys, values, grads, recv), LIMITS["local"], 4 * unit,
        far=(1, 2, 3, 4, 5), far_out=(0, 1, 2), smem=(0,),
        scratch=(
            vmem(2 * tokens, part, dtype=f32), vmem(*pair_tiles.shape), vmem(*pair_tiles.shape),
            sems(8 * part_groups), sems(3 * part_groups),
        ),
    )
    (running,) = call(
        prior_kernel, (half_states,), (place, kv_parts, kv_totals, qg), LIMITS["prior"],
        far=(3,), smem=(0,),
    )
    prior = exchange(running, "inner", pair_groups)
    (gq_state,) = call(
        mixed_kernel, (half_states,), (qg, inner, prior), LIMITS["mixed"], 2 * unit,
        far_out=(0,), scratch=(vmem(*half_states.shape), sems(part_groups)),
    )
    gq_parts = exchange(gq_state, "inner", pair_groups)
    swapped = shape(4, tokens, part)
    own, send = call(
        side_kernel, (swapped, swapped), (core, qg, kv_pair, inner, prior), LIMITS["side"], 10 * unit,
        far=(1, 2, 3, 4), far_out=(0, 1), smem=(0,),
        scratch=(
            vmem(*pair_tiles.shape), vmem(*pair_tiles.shape), vmem(2 * tokens, part, dtype=f32),
            vmem(*half_states.shape), vmem(4, 2 * tokens, part),
            sems(3 * part_groups), sems(1), sems(8 * part_groups),
        ),
    )
    (sent,) = call(total_kernel, totals_shape, (gq_parts, own), LIMITS["total"], far=(1,))
    gq_totals = exchange(sent, "outer", outer_groups)
    (running,) = call(
        later_kernel, (states,), (place, gq_parts, gq_totals), LIMITS["later"],
        far_out=(0,), smem=(0,), scratch=(vmem(*states.shape), sems(4)),
    )
    later = exchange(running.reshape(-1, slice_rows, HEAD_DIM), "inner", inner_groups)
    recv = lax.ppermute(send, "inner", swap)
    attended, grad_query = call(
        finish_kernel, (out, out), (core, own, recv), LIMITS["finish"],
        far=(1, 2), smem=(0,), scratch=(sems(4),),
    )
    grad_key, grad_value = call(
        last_kernel, (out, out), (core, keys, values, own, recv, later), LIMITS["last"], 2 * unit,
        far=(3, 4, 5), far_out=(0, 1), smem=(0,),
        scratch=(rows, rows, vmem(*later.shape), rows, rows, sems(4), sems(1), sems(2 * groups)),
    )
    return attended, grad_query, grad_key, grad_value


def solution(mesh):
    split = Mesh(mesh.devices.reshape(-1, 64), ("outer", "inner"))
    placed = P(("outer", "inner"), None)
    return jax.shard_map(
        per_device,
        mesh=split,
        in_specs=(placed,) * 4,
        out_specs=(placed,) * 4,
        check_vma=False,
    )
```

```python
import functools

import jax
import jax.numpy as jnp
from jax import lax
from jax.experimental import pallas as pl
from jax.experimental.pallas import tpu as pltpu
from jax.sharding import Mesh, PartitionSpec as P

HEAD_DIM = 128
GROUP = 512
MIB = 1024 * 1024
LIMITS = {
    "state": 53 * MIB,
    "pack": 56 * MIB,
    "total": 53 * MIB,
    "local": 51 * MIB,
    "prior": 53 * MIB,
    "mixed": 50 * MIB,
    "side": 56 * MIB,
    "later": 53 * MIB,
    "finish": 48 * MIB,
    "last": 50 * MIB,
}
OUTER_TURN = 5
INNER_TURN = 53
PAIR_TURN, CORE_TURN = INNER_TURN // 2, INNER_TURN % 2
f32 = jnp.float32
bf16 = jnp.bfloat16


def dot_nn(a, b):
    return lax.dot_general(a, b, (((1,), (0,)), ((), ())), preferred_element_type=f32)


def dot_nt(a, b):
    return lax.dot_general(a, b, (((1,), (1,)), ((), ())), preferred_element_type=f32)


def dot_tn(a, b):
    return lax.dot_general(a, b, (((0,), (0,)), ((), ())), preferred_element_type=f32)


def shape(*dims, dtype=bf16):
    return jax.ShapeDtypeStruct(dims, dtype)


def call(kernel, out_shape, operands, limit, flops=0, far=(), far_out=(), smem=(), scratch=()):
    def space(i, kept):
        return pl.BlockSpec(memory_space=pltpu.HBM if i in kept else pltpu.VMEM)

    in_specs = [
        pl.BlockSpec(memory_space=pltpu.SMEM) if i in smem else space(i, far)
        for i in range(len(operands))
    ]
    out_specs = tuple(space(i, far_out) for i in range(len(out_shape)))
    moved = sum(x.size * x.dtype.itemsize for x in tuple(operands) + out_shape)
    return pl.pallas_call(
        kernel,
        out_shape=out_shape,
        in_specs=in_specs,
        out_specs=out_specs,
        scratch_shapes=scratch,
        compiler_params=pltpu.CompilerParams(vmem_limit_bytes=limit),
        cost_estimate=pl.CostEstimate(flops=flops, bytes_accessed=moved, transcendentals=0),
    )(*operands)


def copies_of(pairs, sems, first=0):
    return [
        pltpu.make_async_copy(src, dst, sems.at[first + i]) for i, (src, dst) in enumerate(pairs)
    ]


def start_all(copies):
    for copy in copies:
        copy.start()


def wait_all(copies):
    for copy in copies:
        copy.wait()


def columns(g, width=GROUP):
    return pl.ds(g * width, width)


def heads_of(g, width=GROUP):
    heads = range(g * width // HEAD_DIM, (g + 1) * width // HEAD_DIM)
    return [(h, slice(h * HEAD_DIM, (h + 1) * HEAD_DIM)) for h in heads]


def half(ref, which):
    count = ref.shape[-1] // 2
    return ref.at[:, pl.ds(pl.multiple_of(which * count, count), count)]


def rows_of(core, count):
    return pl.ds(pl.multiple_of(core * count, count), count)


def turned_block(g, size):
    return pl.ds((g * size) ^ (PAIR_TURN // size * size), size)


def at_or_after(count, turned=False):
    rows = lax.broadcasted_iota(jnp.int32, (count, count), 0)
    cols = lax.broadcasted_iota(jnp.int32, (count, count), 1)
    return cols >= rows if turned else rows >= cols


def state_kernel(k_far, v_far, out_far, k_ref, v_ref, out_ref, sems, out_sems):
    pairs, _, rows, _ = out_far.shape
    cuts = HEAD_DIM // rows
    heads = pairs // cuts
    count = k_far.shape[1] // GROUP
    copies = [
        copies_of(
            [(src.at[:, columns(g)], dst.at[:, columns(g)]) for src, dst in ((k_far, k_ref), (v_far, v_ref))],
            sems, 2 * g,
        )
        for g in range(count)
    ]
    for group in copies:
        start_all(group)
    out_copies = []
    for g, group in enumerate(copies):
        wait_all(group)
        for h, cols in heads_of(g):
            state = dot_tn(k_ref[:, cols], v_ref[:, cols]).astype(bf16)
            for q in range(cuts):
                r = (h % heads) * cuts + q
                out_ref[r ^ PAIR_TURN, h // heads ^ CORE_TURN] = state[q * rows : (q + 1) * rows]
        block, core = turned_block(g % 2, pairs // 2), g // 2 ^ CORE_TURN
        out_copies += copies_of(
            [(out_ref.at[block, core], out_far.at[block, core])], out_sems, g
        )
        out_copies[-1].start()
    wait_all(out_copies)


def total_kernel(parts_ref, after_far, out_ref):
    total = parts_ref[0].astype(f32)
    for j in range(1, parts_ref.shape[0]):
        total = total + parts_ref[j].astype(f32)
    total = total.astype(bf16)
    for j in range(out_ref.shape[0]):
        out_ref[j] = total


def outer_sum(reverse, place, totals_ref):
    acc = jnp.zeros(totals_ref.shape[1:], f32)
    for b in range(totals_ref.shape[0]):
        wanted = b > place if reverse else b < place
        acc = acc + jnp.where(wanted, totals_ref[b ^ OUTER_TURN].astype(f32), 0.0)
    return acc


def prior_kernel(place_ref, parts_ref, totals_ref, after_far, out_ref):
    acc = outer_sum(False, place_ref[0], totals_ref)
    for r in range(out_ref.shape[0]):
        out_ref[r ^ PAIR_TURN] = acc.astype(bf16)
        for i in (2 * r, 2 * r + 1):
            acc = acc + parts_ref[i ^ INNER_TURN].astype(f32)


def later_kernel(place_ref, parts_ref, totals_ref, out_far, out_ref, out_sems):
    acc = outer_sum(True, place_ref[0], totals_ref)
    pairs = parts_ref.shape[0]
    step = pairs // 4
    out_copies = []
    for r in reversed(range(pairs)):
        for c in range(2):
            out_ref[r ^ PAIR_TURN, c] = acc.astype(bf16)
        acc = acc + parts_ref[r ^ PAIR_TURN].astype(f32)
        if r % step == 0:
            block = pl.ds((r ^ PAIR_TURN) // step * step, step)
            out_copies += copies_of([(out_ref.at[block], out_far.at[block])], out_sems, r // step)
            out_copies[-1].start()
    wait_all(out_copies)


def pack_kernel(core_ref, q_far, k_far, v_far, g_far, out_far, near_ref, sems, out_sems):
    other = 1 - core_ref[0]
    rows = (q_far, k_far, v_far, g_far)
    copies = copies_of([(half(src, other), near_ref.at[i]) for i, src in enumerate(rows)], sems)
    start_all(copies)
    out_copies = copies_of([(near_ref.at[i], out_far.at[i]) for i in range(len(rows))], out_sems)
    for copy, out_copy in zip(copies, out_copies):
        copy.wait()
        out_copy.start()
    wait_all(out_copies)


def local_kernel(
    core_ref, q_far, k_far, v_far, g_far, recv_far, inner_far, qg_far, kv_far,
    inner_ref, qg_ref, kv_ref, sems, out_sems,
):
    core = core_ref[0]
    count = q_far.shape[0]
    part = inner_far.shape[1]
    mine, theirs = rows_of(core, count), rows_of(1 - core, count)
    q_ref, k_ref, v_ref = qg_ref.at[0], kv_ref.at[0], kv_ref.at[1]
    near = (q_ref, k_ref, v_ref, qg_ref.at[1])
    copies = []
    for g in range(part // GROUP):
        own = pl.ds(pl.multiple_of(core * part + g * GROUP, GROUP), GROUP)
        pairs = [
            (src.at[:, own], dst.at[mine, columns(g)])
            for src, dst in zip((q_far, k_far, v_far, g_far), near)
        ]
        pairs += [(recv_far.at[i, :, columns(g)], dst.at[theirs, columns(g)]) for i, dst in enumerate(near)]
        copies.append(copies_of(pairs, sems, 8 * g))
    for group in copies:
        start_all(group)
    mask = at_or_after(2 * count)
    out_copies = []
    for g, group in enumerate(copies):
        wait_all(group)
        rows = copies_of(
            [(ref.at[:, :, columns(g)], far.at[:, :, columns(g)]) for ref, far in ((qg_ref, qg_far), (kv_ref, kv_far))],
            out_sems, 3 * g,
        )
        start_all(rows)
        heads = heads_of(g)
        scores = [dot_nt(q_ref[:, cols], k_ref[:, cols]) for _, cols in heads]
        local = [jnp.where(mask, x, 0.0).astype(bf16) for x in scores]
        for (_, cols), x in zip(heads, local):
            inner_ref[:, cols] = dot_nn(x, v_ref[:, cols])
        mixed = copies_of([(inner_ref.at[:, columns(g)], inner_far.at[:, columns(g)])], out_sems, 3 * g + 2)
        start_all(mixed)
        out_copies += rows + mixed
    wait_all(out_copies)


def whole_state(ref, h):
    cuts = HEAD_DIM // ref.shape[1]
    return jnp.concatenate([ref[(h * cuts + q) ^ PAIR_TURN] for q in range(cuts)], axis=0)


def normed_parts(mixed, grad):
    scale = lax.rsqrt(jnp.mean(mixed * mixed, axis=-1, keepdims=True) + 1e-06)
    inner_mean = jnp.mean(grad * mixed, axis=-1, keepdims=True)
    dy = (scale * grad - mixed * (scale * scale * scale * inner_mean)).astype(bf16)
    return scale, dy


def mixed_kernel(qg_ref, inner_ref, prior_ref, state_far, state_ref, out_sems):
    pairs, rows, _ = state_ref.shape
    cuts = HEAD_DIM // rows
    q_ref, g_ref = qg_ref.at[0], qg_ref.at[1]
    count = q_ref.shape[1] // GROUP
    out_copies = []
    for g in range(count):
        for h, cols in heads_of(g):
            query = q_ref[:, cols]
            mixed = inner_ref[:, cols] + dot_nn(query, whole_state(prior_ref, h))
            _, dy = normed_parts(mixed, g_ref[:, cols].astype(f32))
            state = dot_tn(query, dy).astype(bf16)
            for q in range(cuts):
                state_ref[(h * cuts + q) ^ PAIR_TURN] = state[q * rows : (q + 1) * rows]
        block = turned_block(g, pairs // count)
        out_copies += copies_of([(state_ref.at[block], state_far.at[block])], out_sems, g)
        out_copies[-1].start()
    wait_all(out_copies)


def side_kernel(
    core_ref, qg_far, kv_far, inner_far, prior_far, own_far, send_far,
    qg_ref, kv_ref, inner_ref, prior_ref, tile_ref, sems, prior_sem, out_sems,
):
    core = core_ref[0]
    count = own_far.shape[1]
    q_ref, g_ref, k_ref, v_ref = qg_ref.at[0], qg_ref.at[1], kv_ref.at[0], kv_ref.at[1]
    prior_copy = copies_of([(prior_far, prior_ref)], prior_sem)
    start_all(prior_copy)
    copies = [
        copies_of(
            [
                (qg_far.at[:, :, columns(g)], qg_ref.at[:, :, columns(g)]),
                (inner_far.at[:, columns(g)], inner_ref.at[:, columns(g)]),
                (kv_far.at[:, :, columns(g)], kv_ref.at[:, :, columns(g)]),
            ],
            sems, 3 * g,
        )
        for g in range(inner_ref.shape[1] // GROUP)
    ]
    for group in copies:
        start_all(group)
    mask = at_or_after(2 * count)
    turned = at_or_after(2 * count, True)
    mine, theirs = rows_of(core, count), rows_of(1 - core, count)
    wait_all(prior_copy)
    out_copies = []
    for g, group in enumerate(copies):
        wait_all(group)
        heads = heads_of(g)
        queries = [q_ref[:, cols] for _, cols in heads]
        key_rows = [k_ref[:, cols] for _, cols in heads]
        value_rows = [v_ref[:, cols] for _, cols in heads]
        priors = [whole_state(prior_ref, h) for h, _ in heads]
        mixed = [inner_ref[:, cols] + dot_nn(q, p) for (_, cols), q, p in zip(heads, queries, priors)]
        local_t = [
            jnp.where(turned, dot_nt(k, q), 0.0).astype(bf16) for k, q in zip(key_rows, queries)
        ]
        normed = [normed_parts(x, g_ref[:, cols].astype(f32)) for x, (_, cols) in zip(mixed, heads)]
        dlocal = [
            jnp.where(mask, dot_nt(dy, v), 0.0).astype(bf16) for (_, dy), v in zip(normed, value_rows)
        ]
        dlocal_t = [
            jnp.where(turned, dot_nt(v, dy), 0.0).astype(bf16) for (_, dy), v in zip(normed, value_rows)
        ]
        results = (
            lambda i: mixed[i] * normed[i][0],
            lambda i: dot_nn(dlocal[i], key_rows[i]) + dot_nt(normed[i][1], priors[i]),
            lambda i: dot_nn(dlocal_t[i], queries[i]),
            lambda i: dot_nn(local_t[i], normed[i][1]),
        )
        for slot, result in enumerate(results):
            for i, (_, cols) in enumerate(heads):
                tile_ref[slot, :, cols] = result(i).astype(bf16)
            slot_out = copies_of(
                [
                    (tile_ref.at[slot, mine, columns(g)], own_far.at[slot, :, columns(g)]),
                    (tile_ref.at[slot, theirs, columns(g)], send_far.at[slot, :, columns(g)]),
                ],
                out_sems, 2 * (len(results) * g + slot),
            )
            start_all(slot_out)
            out_copies += slot_out
    wait_all(out_copies)


def swapped_copies(core, first, outs, own_far, recv_far, sems):
    pairs = [(own_far.at[first + i], half(dst, core)) for i, dst in enumerate(outs)]
    pairs += [(recv_far.at[first + i], half(dst, 1 - core)) for i, dst in enumerate(outs)]
    return copies_of(pairs, sems)


def finish_kernel(core_ref, own_far, recv_far, attended_ref, gq_ref, sems):
    copies = swapped_copies(core_ref[0], 0, (attended_ref, gq_ref), own_far, recv_far, sems)
    start_all(copies)
    wait_all(copies)


def last_kernel(
    core_ref, k_ref, v_ref, own_far, recv_far, later_far, out_k_far, out_v_far,
    gk_ref, gv_ref, later_ref, out_k_ref, out_v_ref, sems, later_sem, out_sems,
):
    cuts = HEAD_DIM // later_far.shape[1]
    heads = later_far.shape[0] // cuts // 2
    copies = copies_of([(later_far, later_ref)], later_sem)
    copies += swapped_copies(core_ref[0], 2, (gk_ref, gv_ref), own_far, recv_far, sems)
    start_all(copies)
    wait_all(copies)
    out_copies = []
    for g in range(k_ref.shape[1] // GROUP):
        for h, cols in heads_of(g):
            places = [2 * ((h % heads) * cuts + q) + h // heads for q in range(cuts)]
            later = jnp.concatenate([later_ref[i ^ INNER_TURN] for i in places], axis=0)
            gk = gk_ref[:, cols].astype(f32) + dot_nt(v_ref[:, cols], later)
            gv = gv_ref[:, cols].astype(f32) + dot_nn(k_ref[:, cols], later)
            out_k_ref[:, cols] = gk.astype(bf16)
            out_v_ref[:, cols] = gv.astype(bf16)
        group = copies_of(
            [
                (near.at[:, columns(g)], far.at[:, columns(g)])
                for near, far in ((out_k_ref, out_k_far), (out_v_ref, out_v_far))
            ],
            out_sems, 2 * g,
        )
        start_all(group)
        out_copies += group
    wait_all(out_copies)


def exchange(blocks, axis, groups):
    return lax.all_to_all(blocks, axis, 0, 0, tiled=True, axis_index_groups=groups)


def per_device(query, keys, values, grads):
    tokens, width = query.shape
    part = width // 2
    pairs = lax.axis_size("inner") // 2
    blocks = lax.axis_size("outer")
    slice_rows = part // pairs
    groups = width // GROUP
    part_groups = part // GROUP
    unit = 2 * tokens * width * HEAD_DIM
    core = (lax.axis_index("inner").astype(jnp.int32) % 2).reshape(1)
    place = lax.axis_index("outer").astype(jnp.int32).reshape(1)
    swap = [(i, i ^ 1) for i in range(2 * pairs)]
    outer_groups = [[b ^ OUTER_TURN for b in range(blocks)]]
    inner_groups = [[i ^ INNER_TURN for i in range(2 * pairs)]]
    pair_groups = [[2 * (r ^ PAIR_TURN) + c for r in range(pairs)] for c in range(2)]

    def vmem(*dims, dtype=bf16):
        return pltpu.VMEM(dims, dtype)

    def sems(count):
        return pltpu.SemaphoreType.DMA((count,))

    rows = vmem(tokens, width)
    totals_shape = (shape(blocks, slice_rows, HEAD_DIM),)
    half_states = shape(pairs, slice_rows, HEAD_DIM)
    states = shape(pairs, 2, slice_rows, HEAD_DIM)
    pair_tiles = shape(2, 2 * tokens, part)
    inner_shape = shape(2 * tokens, part, dtype=f32)
    out = shape(tokens, width)

    (kv,) = call(
        state_kernel, (states,), (keys, values), LIMITS["state"], unit,
        far=(0, 1), far_out=(0,),
        scratch=(rows, rows, vmem(*states.shape), sems(2 * groups), sems(groups)),
    )
    kv_parts = exchange(kv.reshape(-1, slice_rows, HEAD_DIM), "inner", inner_groups)
    (send,) = call(
        pack_kernel, (shape(4, tokens, part),), (core, query, keys, values, grads), LIMITS["pack"],
        far=(1, 2, 3, 4), far_out=(0,), smem=(0,),
        scratch=(vmem(4, tokens, part), sems(4), sems(4)),
    )
    recv = lax.ppermute(send, "inner", swap)
    (sent,) = call(total_kernel, totals_shape, (kv_parts, send), LIMITS["total"], far=(1,))
    kv_totals = exchange(sent, "outer", outer_groups)
    inner, qg, kv_pair = call(
        local_kernel, (inner_shape, pair_tiles, pair_tiles),
        (core, query, keys, values, grads, recv), LIMITS["local"], 4 * unit,
        far=(1, 2, 3, 4, 5), far_out=(0, 1, 2), smem=(0,),
        scratch=(
            vmem(2 * tokens, part, dtype=f32), vmem(*pair_tiles.shape), vmem(*pair_tiles.shape),
            sems(8 * part_groups), sems(3 * part_groups),
        ),
    )
    (running,) = call(
        prior_kernel, (half_states,), (place, kv_parts, kv_totals, qg), LIMITS["prior"],
        far=(3,), smem=(0,),
    )
    prior = exchange(running, "inner", pair_groups)
    (gq_state,) = call(
        mixed_kernel, (half_states,), (qg, inner, prior), LIMITS["mixed"], 2 * unit,
        far_out=(0,), scratch=(vmem(*half_states.shape), sems(part_groups)),
    )
    gq_parts = exchange(gq_state, "inner", pair_groups)
    swapped = shape(4, tokens, part)
    own, send = call(
        side_kernel, (swapped, swapped), (core, qg, kv_pair, inner, prior), LIMITS["side"], 10 * unit,
        far=(1, 2, 3, 4), far_out=(0, 1), smem=(0,),
        scratch=(
            vmem(*pair_tiles.shape), vmem(*pair_tiles.shape), vmem(2 * tokens, part, dtype=f32),
            vmem(*half_states.shape), vmem(4, 2 * tokens, part),
            sems(3 * part_groups), sems(1), sems(8 * part_groups),
        ),
    )
    (sent,) = call(total_kernel, totals_shape, (gq_parts, own), LIMITS["total"], far=(1,))
    gq_totals = exchange(sent, "outer", outer_groups)
    (running,) = call(
        later_kernel, (states,), (place, gq_parts, gq_totals), LIMITS["later"],
        far_out=(0,), smem=(0,), scratch=(vmem(*states.shape), sems(4)),
    )
    later = exchange(running.reshape(-1, slice_rows, HEAD_DIM), "inner", inner_groups)
    recv = lax.ppermute(send, "inner", swap)
    attended, grad_query = call(
        finish_kernel, (out, out), (core, own, recv), LIMITS["finish"],
        far=(1, 2), smem=(0,), scratch=(sems(4),),
    )
    grad_key, grad_value = call(
        last_kernel, (out, out), (core, keys, values, own, recv, later), LIMITS["last"], 2 * unit,
        far=(3, 4, 5), far_out=(0, 1), smem=(0,),
        scratch=(rows, rows, vmem(*later.shape), rows, rows, sems(4), sems(1), sems(2 * groups)),
    )
    return attended, grad_query, grad_key, grad_value


def solution(mesh):
    split = Mesh(mesh.devices.reshape(-1, 64), ("outer", "inner"))
    placed = P(("outer", "inner"), None)
    return jax.shard_map(
        per_device,
        mesh=split,
        in_specs=(placed,) * 4,
        out_specs=(placed,) * 4,
        check_vma=False,
    )
```
